32 devices in a mesh: tok: 8 (over z, x), feat: 4 (over y, core).
Axes of the slice: x: 2, y: 2, z: 4, core: 2. Of those that a mesh axis runs over, the one named last changes fastest.
Arguments:
- patches: bfloat16 [96, 6144], P('tok', 'feat'), may hold values from -640 to 640
- frame_counts: int32 [8], P('tok'), may hold values from 1 to 3
- patch_mask: int32 [96], P('tok'), may hold values 0 or 1
- norm_gain: float32 [6144], P('feat'), may hold values from 0.1 to 1.9
- up_weight: bfloat16 [6144, 24576], P('feat', 'tok'), may hold values from -0.078125 to 0.078125
- up_bias: float32 [24576], P('tok'), may hold values from -3 to 3
- down_weight: bfloat16 [24576, 6144], P('tok', 'feat'), may hold values from -0.0390625 to 0.0390625
- down_bias: float32 [6144], P('feat'), may hold values from -3 to 3
Outputs:
- block_output: bfloat16 [96, 6144], P('tok', 'feat')
The draws below stay inside these ranges and needn't reach their ends.
All inputs are finite; a program needn't handle non-finite values. No bound on the sum of `patch_mask` on one device may be relied on, other than what follows from the above.
Results may differ from the reference program's by a relative error of at most 0.0053.
Values may be sent and summed in bfloat16 or wider, within the bound.
No kernel may reach another device: no remote copies, remote signals or barrier semaphores. Data moves between devices by JAX's collectives and lax.ppermute only.
A program may use at most 64 MiB of HBM per device.

```python
import jax
import jax.numpy as jnp
from jax import lax

D = 6144
FF = 24576
FRAME_TOK = 4
FRAMES = 3
TOK_DEV = 12
CLIPS = 8
TOKENS = 96


def draw_patches(key, part):
    first_key, second_key = jax.random.split(key, 2)
    column = jnp.arange(D, dtype=jnp.float32) / D
    row_scale = 10.0 ** jax.random.uniform(second_key, (TOKENS, 1), dtype=jnp.float32)
    base = jax.random.normal(first_key, (TOKENS, D), dtype=jnp.float32)
    col_scale = 10.0 ** column
    return (base * col_scale[None, :] * row_scale).astype(jnp.bfloat16)


def plant(entries, own_key, smallest, high):
    index_at = [jax.random.randint(jax.random.fold_in(own_key, axis), (), 0, length) for axis, length in enumerate(entries.shape)]
    widest = entries.shape.index(max(entries.shape))
    next_to = index_at[:widest] + [(index_at[widest] + 1) % entries.shape[widest]] + index_at[widest + 1:]
    return entries.at[tuple(index_at)].set(smallest).at[tuple(next_to)].set(high)


def block_levels(rng, shape, pieces, smallest, top_value):
    def one(axis_at, parts):
        draws = jax.random.uniform(jax.random.fold_in(jax.random.fold_in(rng, 6), axis_at), (parts,), jnp.float32, smallest / len(pieces), top_value / len(pieces))
        return jnp.repeat(jnp.exp(draws), shape[axis_at] // parts).reshape((-1,) + (1,) * (len(shape) - axis_at - 1))

    loudness = one(*pieces[0])
    for cut in pieces[1:]:
        loudness = loudness * one(*cut)
    return loudness


def normal_values(rng, dims, deviation, reach, pieces=(), kind=jnp.bfloat16):
    values = jax.random.normal(rng, dims, jnp.float32) * deviation
    if len(pieces) > 0:
        values = block_levels(rng, dims, pieces, -0.22, 0.18) * values
    return jnp.clip(values, min=-reach, max=reach).astype(kind)


def setup_inputs(seed: int = 0) -> dict:
    key_of = jax.random.split(jax.random.key(seed), 9)
    patches = draw_patches(jax.random.fold_in(key_of[8], 71), 0)
    frame_counts = plant(jax.random.randint(key_of[1], (CLIPS,), 1, FRAMES + 1), jax.random.fold_in(key_of[1], 1), 1, FRAMES).astype(jnp.int32)
    patch_mask = plant((jax.random.randint(key_of[2], (TOKENS,), 0, 8) < 7).astype(jnp.int32), jax.random.fold_in(key_of[2], 1), 0, 1)
    norm_gain = jnp.clip(1.0 + 0.18 * jax.random.normal(key_of[3], (D,), jnp.float32), 0.1, 1.9)
    up_weight = normal_values(key_of[4], (D, FF), D ** -0.5, 0.078125, ((0, 4), (1, 8)))
    up_bias = normal_values(key_of[5], (FF,), 0.5, 3.0, ((0, 8),), jnp.float32)
    down_weight = normal_values(key_of[6], (FF, D), FF ** -0.5, 0.0390625, ((0, 8), (1, 4)))
    down_bias = normal_values(key_of[7], (D,), 0.5, 3.0, ((0, 4),), jnp.float32)
    return {"patches": patches, "frame_counts": frame_counts, "patch_mask": patch_mask, "norm_gain": norm_gain, "up_weight": up_weight, "up_bias": up_bias, "down_weight": down_weight, "down_bias": down_bias}


epsilon = 1e-06

def reference(patches, frame_counts, patch_mask, norm_gain, up_weight, up_bias, down_weight, down_bias):
    values = patches.astype(jnp.float32)
    row_mean = lax.optimization_barrier(jnp.sum(values, axis=1)) / D
    spread = lax.optimization_barrier(jnp.sum(values * values, axis=1)) / D - row_mean * row_mean
    scaled = (values - row_mean[:, None]) * lax.rsqrt(spread + epsilon)[:, None]
    normed = (scaled * norm_gain[None, :]).astype(jnp.bfloat16)
    preact = jnp.dot(normed, up_weight, preferred_element_type=jnp.float32) + up_bias[None, :]
    hidden = jax.nn.gelu(preact, approximate=True).astype(jnp.bfloat16)
    summed = jnp.dot(hidden, down_weight, preferred_element_type=jnp.float32) + down_bias[None, :]
    positions = jnp.arange(TOKENS, dtype=jnp.int32)
    limits = jnp.repeat(frame_counts.astype(jnp.int32), TOK_DEV, total_repeat_length=TOKENS)
    valid_rows = ((positions % TOK_DEV // FRAME_TOK < limits) & (patch_mask == 1)).astype(jnp.float32)
    return (valid_rows[:, None] * summed).astype(jnp.bfloat16)
```

```python
import jax
import jax.numpy as jnp
from jax import lax
from jax.sharding import PartitionSpec as P

FRAME_TOK = 4

epsilon = 1e-06


def swap(block, axis, mask):
    size = lax.axis_size(axis)
    return lax.ppermute(block, axis, [(i, i ^ mask) for i in range(size)])


def per_device(
    patches, frame_counts, patch_mask, norm_gain, up_weight, up_bias, down_weight, down_bias
):
    tok_rows = patches.shape[0]
    tok_size = lax.axis_size("tok")
    feat_size = lax.axis_size("feat")
    full_width = patches.shape[1] * feat_size
    first_core = lax.axis_index("feat") % 2 == 0

    values = patches.astype(jnp.float32)
    sums = jnp.stack([jnp.sum(values, axis=1), jnp.sum(values * values, axis=1)])
    parts = [swap(sums, "feat", mask) for mask in range(1, feat_size)]
    for part in parts:
        sums = sums + part
    row_mean = sums[0] / full_width
    spread = sums[1] / full_width - row_mean * row_mean
    scaled = (values - row_mean[:, None]) * lax.rsqrt(spread + epsilon)[:, None]
    normed = (scaled * norm_gain[None, :]).astype(jnp.bfloat16)

    masks = range(2, tok_size, 2)
    near = jnp.concatenate([normed] + [swap(normed, "tok", mask) for mask in masks])
    far = swap(near, "tok", 1)
    half = near.shape[0]

    kept = jnp.where(first_core, near, far)
    given = jnp.where(first_core, far, near)
    product = jnp.dot(
        jnp.concatenate([kept, given]), up_weight, preferred_element_type=jnp.float32
    )
    preact = product[:half] + swap(product[half:].astype(jnp.bfloat16), "feat", 1)
    sent = preact.astype(jnp.bfloat16)
    for part in [swap(sent, "feat", mask) for mask in range(2, feat_size, 2)]:
        preact = preact + part
    active = jax.nn.gelu(preact + up_bias[None, :], approximate=True).astype(jnp.bfloat16)
    hidden = jnp.concatenate([active, swap(active, "feat", 1)])
    product = jnp.dot(hidden, down_weight, preferred_element_type=jnp.float32)

    near_sum = jnp.where(first_core, product[:half], product[half:])
    far_sum = jnp.where(first_core, product[half:], product[:half])
    near_sum = near_sum + swap(far_sum.astype(jnp.bfloat16), "tok", 1)
    blocks = near_sum.reshape(tok_size // 2, tok_rows, near_sum.shape[1])
    summed = blocks[0]
    sent = blocks.astype(jnp.bfloat16)
    for part in [swap(sent[mask // 2], "tok", mask) for mask in masks]:
        summed = summed + part

    positions = jnp.arange(tok_rows, dtype=jnp.int32)
    valid_rows = ((positions // FRAME_TOK < frame_counts[0]) & (patch_mask == 1)).astype(
        jnp.float32
    )
    return (valid_rows[:, None] * (summed + down_bias[None, :])).astype(jnp.bfloat16)


def solution(mesh):
    in_specs = (
        P("tok", "feat"),
        P("tok"),
        P("tok"),
        P("feat"),
        P("feat", "tok"),
        P("tok"),
        P("tok", "feat"),
        P("feat"),
    )
    out_specs = P("tok", "feat")
    return jax.shard_map(
        per_device, mesh=mesh, in_specs=in_specs, out_specs=out_specs, check_vma=False
    )
```

```python
import jax
import jax.numpy as jnp
from jax import lax
from jax.experimental import pallas as pl
from jax.experimental.pallas import tpu as pltpu
from jax.sharding import PartitionSpec as P

FRAME_TOK = 4
LANES = 128
MIB = 2**20

epsilon = 1e-06

in_vmem = pl.BlockSpec(memory_space=pltpu.VMEM)


def swap(block, axis, mask):
    size = lax.axis_size(axis)
    return lax.ppermute(block, axis, [(i, i ^ mask) for i in range(size)])


def is_first_core():
    return lax.rem(lax.axis_index("feat"), 2) == 0


def tile_of(width):
    return next((t for t in (512, 384, 256, 128) if width % t == 0), width)


def call(kernel, outs, in_specs, scratch=(), flops=0, limit=4):
    outs = [jax.ShapeDtypeStruct(shape, dtype) for shape, dtype in outs]
    return pl.pallas_call(
        kernel,
        out_shape=outs,
        in_specs=in_specs,
        out_specs=[in_vmem] * len(outs),
        scratch_shapes=list(scratch),
        compiler_params=pltpu.CompilerParams(vmem_limit_bytes=limit * MIB),
        cost_estimate=pl.CostEstimate(
            flops=flops, bytes_accessed=sum(o.size * 4 for o in outs), transcendentals=0
        ),
    )


def pieces(column):
    high = column.astype(jnp.bfloat16).astype(jnp.float32)
    middle = (column - high).astype(jnp.bfloat16).astype(jnp.float32)
    return high, middle, column - high - middle


def pack(sums, squares):
    lane = lax.broadcasted_iota(jnp.int32, (sums.shape[0], LANES), 1)
    packed = jnp.zeros((sums.shape[0], LANES), jnp.float32)
    for at, piece in enumerate(pieces(sums) + pieces(squares)):
        packed = jnp.where(lane == at, piece, packed)
    return packed.astype(jnp.bfloat16)


def unpack(packed):
    packed = packed.astype(jnp.float32)
    column = [packed[:, at:at + 1] for at in range(6)]
    return column[0] + column[1] + column[2], column[3] + column[4] + column[5]


def gain_kernel(gain_ref, weight_ref, row_ref):
    width = weight_ref.shape[1]
    tile = tile_of(width)
    gain = gain_ref[...]
    high = gain.astype(jnp.bfloat16).astype(jnp.float32)
    row = lax.broadcasted_iota(jnp.int32, (16, gain.shape[1]), 0)
    rows = jnp.where(row == 0, high, jnp.where(row == 1, gain - high, 0.0)).astype(jnp.bfloat16)
    for at in range(0, width, tile):
        product = jnp.dot(rows, weight_ref[:, at:at + tile], preferred_element_type=jnp.float32)
        row_ref[:, at:at + tile] = product[0:1] + product[1:2]


def up_kernel(near_ref, far_ref, gain_ref, weight_ref, kept_ref, given_ref, own_ref, rows_ref):
    half, block_width = near_ref.shape
    width = weight_ref.shape[1]
    first = is_first_core()
    near, far = near_ref[...].astype(jnp.float32), far_ref[...].astype(jnp.float32)
    for at, values in enumerate((jnp.where(first, near, far), jnp.where(first, far, near))):
        sums = jnp.sum(values, axis=1, keepdims=True)
        squares = jnp.sum(values * values, axis=1, keepdims=True)
        centred = (values - sums / block_width) * gain_ref[...]
        rows_ref[at * half:(at + 1) * half] = centred.astype(jnp.bfloat16)
        packed = pack(sums, squares)
        if at == 0:
            own_ref[...] = packed
        else:
            given_ref[:, width:] = packed
    tile = tile_of(width)
    for at in range(0, width, tile):
        product = jnp.dot(
            rows_ref[...], weight_ref[:, at:at + tile], preferred_element_type=jnp.float32
        )
        kept_ref[:, at:at + tile] = product[:half]
        given_ref[:, at:at + tile] = product[half:].astype(jnp.bfloat16)


def pair_kernel(block_width, kept_ref, own_ref, other_ref, gain_ref, other_gain_ref, sum_ref, sent_ref):
    width = kept_ref.shape[1]
    sums, squares = unpack(own_ref[...])
    other_sums, other_squares = unpack(other_ref[:, width:])
    shift = (sums - other_sums) / (2 * block_width)
    tile = tile_of(width)
    for at in range(0, width, tile):
        cut = slice(at, at + tile)
        gains = gain_ref[:, cut] - other_gain_ref[:, cut]
        total = kept_ref[:, cut] + other_ref[:, cut].astype(jnp.float32) + shift * gains
        sum_ref[:, cut] = total
        sent_ref[:, cut] = total.astype(jnp.bfloat16)
    sent_ref[:, width:] = pack(sums + other_sums, squares + other_squares)


def gelu_kernel(block_width, full_width, peers, bias_ref, sum_ref, sent_ref, gain_ref, *refs):
    others, gains, out_ref = refs[:peers], refs[peers:2 * peers], refs[2 * peers]
    width = sum_ref.shape[1]
    stats = [unpack(ref[:, width:]) for ref in (sent_ref,) + others]
    row_mean = sum(s[0] for s in stats) / full_width
    spread = sum(s[1] for s in stats) / full_width - row_mean * row_mean
    scale = lax.rsqrt(spread + epsilon)
    shifts = [s[0] / (2 * block_width) - row_mean for s in stats]
    tile = tile_of(width)
    for at in range(0, width, tile):
        cut = slice(at, at + tile)
        total = sum_ref[:, cut] + shifts[0] * gain_ref[:, cut]
        for other, gain, shift in zip(others, gains, shifts[1:]):
            total = total + other[:, cut].astype(jnp.float32) + shift * gain[:, cut]
        active = jax.nn.gelu(total * scale + bias_ref[:, cut], approximate=True)
        out_ref[:, cut] = active.astype(jnp.bfloat16)


def down_kernel(kept_ref, given_ref, weight_ref, near_ref, far_ref, rows_ref):
    half = kept_ref.shape[0]
    rows_ref[:half] = kept_ref[...]
    rows_ref[half:] = given_ref[...]
    first = is_first_core()
    width = weight_ref.shape[1]
    tile = tile_of(width)
    for at in range(0, width, tile):
        product = jnp.dot(
            rows_ref[...], weight_ref[:, at:at + tile], preferred_element_type=jnp.float32
        )
        kept, given = product[:half], product[half:]
        near_ref[:, at:at + tile] = jnp.where(first, kept, given)
        far_ref[:, at:at + tile] = jnp.where(first, given, kept).astype(jnp.bfloat16)


def per_device(
    patches, frame_counts, patch_mask, norm_gain, up_weight, up_bias, down_weight, down_bias
):
    tok_rows, block_width = patches.shape
    hidden_width = up_weight.shape[1]
    tok_size = lax.axis_size("tok")
    feat_size = lax.axis_size("feat")
    full_width = block_width * feat_size
    norm_gain = norm_gain[None, :]
    f32, bf16 = jnp.float32, jnp.bfloat16

    masks = range(2, tok_size, 2)
    (gain_row,) = call(
        gain_kernel, [((1, hidden_width), f32)], [in_vmem] * 2, flops=32 * up_weight.size
    )(norm_gain, up_weight)
    near = jnp.concatenate([patches] + [swap(patches, "tok", mask) for mask in masks])
    near, gain_row = lax.optimization_barrier((near, gain_row))
    far = swap(near, "tok", 1)
    half = near.shape[0]
    other_gain = swap(gain_row, "feat", 1)
    pair_gain = gain_row + other_gain
    peers = range(2, feat_size, 2)
    peer_gains = [swap(pair_gain, "feat", mask) for mask in peers]

    kept, given, own = call(
        up_kernel,
        [((half, hidden_width), f32), ((half, hidden_width + LANES), bf16), ((half, LANES), bf16)],
        [in_vmem] * 4,
        [pltpu.VMEM((2 * half, block_width), bf16)],
        flops=4 * half * up_weight.size,
        limit=4,
    )(near, far, norm_gain, up_weight)
    other = swap(given, "feat", 1)
    pair_sum, sent = call(
        lambda *refs: pair_kernel(block_width, *refs),
        [((half, hidden_width), f32), ((half, hidden_width + LANES), bf16)],
        [in_vmem] * 5,
    )(kept, own, other, gain_row, other_gain)
    others = [swap(sent, "feat", mask) for mask in peers]
    (active,) = call(
        lambda *refs: gelu_kernel(block_width, full_width, len(peers), *refs),
        [((half, hidden_width), bf16)],
        [in_vmem] * (4 + 2 * len(peers)),
        limit=4,
    )(up_bias[None, :], pair_sum, sent, pair_gain, *others, *peer_gains)
    near_sum, far_sum = call(
        down_kernel,
        [((half, block_width), f32), ((half, block_width), bf16)],
        [in_vmem] * 3,
        [pltpu.VMEM((2 * half, hidden_width), bf16)],
        flops=4 * half * down_weight.size,
        limit=4,
    )(active, swap(active, "feat", 1), down_weight)

    near_sum = near_sum + swap(far_sum, "tok", 1)
    blocks = near_sum.reshape(tok_size // 2, tok_rows, block_width)
    summed = blocks[0]
    sent = blocks.astype(bf16)
    for part in [swap(sent[mask // 2], "tok", mask) for mask in masks]:
        summed = summed + part

    positions = jnp.arange(tok_rows, dtype=jnp.int32)
    valid_rows = ((positions // FRAME_TOK < frame_counts[0]) & (patch_mask == 1)).astype(f32)
    return (valid_rows[:, None] * (summed + down_bias[None, :])).astype(bf16)


def solution(mesh):
    in_specs = (
        P("tok", "feat"),
        P("tok"),
        P("tok"),
        P("feat"),
        P("feat", "tok"),
        P("tok"),
        P("tok", "feat"),
        P("feat"),
    )
    out_specs = P("tok", "feat")
    return jax.shard_map(
        per_device, mesh=mesh, in_specs=in_specs, out_specs=out_specs, check_vma=False
    )
```

```python
import functools

import jax
import jax.numpy as jnp
from jax import lax
from jax.experimental import pallas as pl
from jax.experimental.pallas import tpu as pltpu
from jax.sharding import PartitionSpec as P

FRAME_TOK = 4
LANES = 128
MIB = 2**20
PARTS = 2

epsilon = 1e-06

in_vmem = pl.BlockSpec(memory_space=pltpu.VMEM)
in_hbm = pl.BlockSpec(memory_space=pltpu.HBM)


def swap(block, axis, mask):
    size = lax.axis_size(axis)
    return lax.ppermute(block, axis, [(i, i ^ mask) for i in range(size)])


def is_first_core():
    return lax.rem(lax.axis_index("feat"), 2) == 0


def tile_of(width):
    return next((t for t in (512, 384, 256, 128) if width % t == 0), width)


def call(kernel, outs, in_specs, scratch=(), flops=0, limit=4):
    outs = [jax.ShapeDtypeStruct(shape, dtype) for shape, dtype in outs]
    return pl.pallas_call(
        kernel,
        out_shape=outs,
        in_specs=in_specs,
        out_specs=[in_vmem] * len(outs),
        scratch_shapes=list(scratch),
        compiler_params=pltpu.CompilerParams(vmem_limit_bytes=limit * MIB),
        cost_estimate=pl.CostEstimate(
            flops=flops, bytes_accessed=sum(o.size * 4 for o in outs), transcendentals=0
        ),
    )


def pieces(column):
    high = column.astype(jnp.bfloat16).astype(jnp.float32)
    middle = (column - high).astype(jnp.bfloat16).astype(jnp.float32)
    return high, middle, column - high - middle


def pack(sums, squares):
    lane = lax.broadcasted_iota(jnp.int32, (sums.shape[0], LANES), 1)
    packed = jnp.zeros((sums.shape[0], LANES), jnp.float32)
    for at, piece in enumerate(pieces(sums) + pieces(squares)):
        packed = jnp.where(lane == at, piece, packed)
    return packed.astype(jnp.bfloat16)


def unpack(packed):
    packed = packed.astype(jnp.float32)
    column = [packed[:, at:at + 1] for at in range(6)]
    return column[0] + column[1] + column[2], column[3] + column[4] + column[5]


def pack_row(row_of, width, scratch, out_ref):
    count = width // LANES
    scratch[...] = jnp.zeros_like(scratch)
    for at in range(count):
        piece = row_of(at * LANES)
        high = piece.astype(jnp.bfloat16).astype(jnp.float32)
        for place, value in ((at, high), (count + at, piece - high)):
            group, line = divmod(place, scratch.shape[0])
            scratch[line:line + 1, group * LANES:(group + 1) * LANES] = value
    out_ref[...] = scratch[...].astype(jnp.bfloat16)


def unpack_row(packed, start, stop, width):
    count = width // LANES
    pieces = []
    for at in range(start // LANES, stop // LANES):
        piece = 0
        for place in (at, count + at):
            group, line = divmod(place, packed.shape[0])
            piece = piece + packed[line:line + 1, group * LANES:(group + 1) * LANES]
        pieces.append(piece)
    return jnp.concatenate(pieces, axis=1)


def load_up_kernel(gain_ref, weight_ref, out_ref, row_ref, packed_ref, scratch, sems):
    width = weight_ref.shape[1]
    tile = tile_of(width)
    copies = [
        pltpu.make_async_copy(
            weight_ref.at[:, pl.ds(at, tile)], out_ref.at[:, pl.ds(at, tile)], sems.at[at // tile]
        )
        for at in range(0, width, tile)
    ]
    for copy in copies:
        copy.start()
    gain = gain_ref[...][None, :]
    high = gain.astype(jnp.bfloat16).astype(jnp.float32)
    row = lax.broadcasted_iota(jnp.int32, (16, gain.shape[1]), 0)
    rows = jnp.where(row == 0, high, jnp.where(row == 1, gain - high, 0.0)).astype(jnp.bfloat16)
    for at, copy in zip(range(0, width, tile), copies):
        copy.wait()
        product = jnp.dot(rows, out_ref[:, at:at + tile], preferred_element_type=jnp.float32)
        row_ref[:, at:at + tile] = product[0:1] + product[1:2]
    pack_row(lambda at: row_ref[:, at:at + LANES], width, scratch, packed_ref)


def up_kernel(start, near_ref, far_ref, gain_ref, packed_ref, weight_ref, rows_ref, own_ref, kept_ref, given_ref):
    half, block_width = near_ref.shape
    width = kept_ref.shape[1]
    first = is_first_core()
    near, far = near_ref[...].astype(jnp.float32), far_ref[...].astype(jnp.float32)
    for at, values in enumerate((jnp.where(first, near, far), jnp.where(first, far, near))):
        sums = jnp.sum(values, axis=1, keepdims=True)
        squares = jnp.sum(values * values, axis=1, keepdims=True)
        centred = (values - sums / block_width) * gain_ref[...][None, :]
        rows_ref[at * half:(at + 1) * half] = centred.astype(jnp.bfloat16)
        packed = pack(sums, squares)
        if at == 0:
            own_ref[...] = packed
        else:
            given_ref[:, width:width + LANES] = packed
    given_ref[:, width + LANES:] = packed_ref[...]
    up_products(start, rows_ref, weight_ref, kept_ref, given_ref)


def up_products(start, rows_ref, weight_ref, kept_ref, given_ref):
    half, width = kept_ref.shape
    tile = tile_of(width)
    for at in range(0, width, tile):
        product = jnp.dot(
            rows_ref[...], weight_ref[:, start + at:start + at + tile], preferred_element_type=jnp.float32
        )
        kept_ref[:, at:at + tile] = product[:half]
        given_ref[:, at:at + tile] = product[half:].astype(jnp.bfloat16)


def pair_kernel(start, full, block_width, kept_ref, own_ref, gain_ref, packed_ref, other_ref, sum_ref, sent_ref, scratch):
    width = kept_ref.shape[1]
    side = other_ref if start == 0 else packed_ref
    sums, squares = unpack(own_ref[...])
    other_sums, other_squares = unpack(side[:, width:width + LANES])
    shift = (sums - other_sums) / (2 * block_width)
    scratch[...] = side[:, width + LANES:].astype(jnp.float32)
    tile = tile_of(width)
    for at in range(0, width, tile):
        cut, there = slice(at, at + tile), slice(start + at, start + at + tile)
        gains = gain_ref[:, there] - unpack_row(scratch, there.start, there.stop, full)
        total = kept_ref[:, cut] + other_ref[:, cut].astype(jnp.float32) + shift * gains
        sum_ref[:, cut] = total
        sent_ref[:, cut] = total.astype(jnp.bfloat16)
    if start == 0:
        sent_ref[:, width:width + LANES] = pack(sums + other_sums, squares + other_squares)
        rows = [gain_ref[:, at:at + LANES] + unpack_row(scratch, at, at + LANES, full) for at in range(0, full, LANES)]
        pack_row(lambda at: rows[at // LANES], full, scratch, sent_ref.at[:, width + LANES:])


def gelu_kernel(start, full, block_width, full_width, peers, bias_ref, sum_ref, *refs):
    out_ref, scratch = refs[-2:]
    packed, others = refs[:peers + 1], refs[peers + 1:-2] or refs[1:peers + 1]
    width = sum_ref.shape[1]
    stats = [unpack(ref[:, width:width + LANES]) for ref in packed]
    row_mean = sum(s[0] for s in stats) / full_width
    spread = sum(s[1] for s in stats) / full_width - row_mean * row_mean
    scale = lax.rsqrt(spread + epsilon)
    shifts = [s[0] / (2 * block_width) - row_mean for s in stats]
    for at, ref in enumerate(packed):
        scratch[at] = ref[:, width + LANES:].astype(jnp.float32)
    tile = tile_of(width)
    for at in range(0, width, tile):
        cut, there = slice(at, at + tile), slice(start + at, start + at + tile)
        total = sum_ref[:, cut]
        for other in others:
            total = total + other[:, cut].astype(jnp.float32)
        for at, shift in enumerate(shifts):
            total = total + shift * unpack_row(scratch.at[at], there.start, there.stop, full)
        active = jax.nn.gelu(total * scale + bias_ref[:, there], approximate=True)
        out_ref[:, cut] = active.astype(jnp.bfloat16)


def down_kernel(start, last, kept_ref, given_ref, weight_ref, *refs):
    half, depth = kept_ref.shape
    rows_ref = refs[-1]
    rows_ref[:half] = kept_ref[...]
    rows_ref[half:] = given_ref[...]
    first = is_first_core()
    width = weight_ref.shape[1]
    tile = tile_of(width)
    for at in range(0, width, tile):
        cut = slice(at, at + tile)
        product = jnp.dot(
            rows_ref[...], weight_ref[start:start + depth, cut], preferred_element_type=jnp.float32
        )
        if start:
            product = product + refs[0][:, cut]
        if last:
            kept, given = product[:half], product[half:]
            refs[-3][:, cut] = jnp.where(first, kept, given)
            refs[-2][:, cut] = jnp.where(first, given, kept).astype(jnp.bfloat16)
        else:
            refs[-2][:, cut] = product


def per_device(
    patches, frame_counts, patch_mask, norm_gain, up_weight, up_bias, down_weight, down_bias
):
    tok_rows, block_width = patches.shape
    hidden_width = up_weight.shape[1]
    tok_size = lax.axis_size("tok")
    feat_size = lax.axis_size("feat")
    full_width = block_width * feat_size
    f32, bf16 = jnp.float32, jnp.bfloat16

    parts = PARTS if hidden_width % (PARTS * LANES) == 0 else 1
    width = hidden_width // parts
    starts = range(0, hidden_width, width)

    masks = range(2, tok_size, 2)
    peers = range(2, feat_size, 2)
    half = tok_rows * tok_size // 2
    side = LANES * -(-2 * hidden_width // (LANES * half))
    extra = [LANES + side if start == 0 else 0 for start in starts]
    loaded, gain_row, gain_packed = call(
        load_up_kernel,
        [(up_weight.shape, bf16), ((1, hidden_width), f32), ((half, side), bf16)],
        [in_vmem, in_hbm],
        [
            pltpu.VMEM((half, side), f32),
            pltpu.SemaphoreType.DMA((hidden_width // tile_of(hidden_width),)),
        ],
        flops=32 * up_weight.size,
        limit=40,
    )(norm_gain, up_weight)
    near = jnp.concatenate([patches] + [swap(patches, "tok", mask) for mask in masks])
    near, gain_row = lax.optimization_barrier((near, gain_row))
    far = swap(near, "tok", 1)

    kepts, givens = [], []
    for start, more in zip(starts, extra):
        outs = [((half, width), f32), ((half, width + more), bf16)]
        flops = 4 * half * block_width * width
        if start == 0:
            rows, own, kept, given = call(
                functools.partial(up_kernel, start),
                [((2 * half, block_width), bf16), ((half, LANES), bf16)] + outs,
                [in_vmem] * 5,
                flops=flops,
            )(near, far, norm_gain, gain_packed, loaded)
        else:
            kept, given = call(
                functools.partial(up_products, start), outs, [in_vmem] * 2, flops=flops
            )(rows, loaded)
        kepts.append(kept)
        givens.append(given)
    others = [swap(given, "feat", 1) for given in givens]
    sums, sents = [], []
    for start, more, kept, other in zip(starts, extra, kepts, others):
        pair_sum, sent = call(
            functools.partial(pair_kernel, start, hidden_width, block_width),
            [((half, width), f32), ((half, width + more), bf16)],
            [in_vmem] * 5,
            [pltpu.VMEM((half, side), f32)],
        )(kept, own, gain_row, others[0], other)
        sums.append(pair_sum)
        sents.append(sent)
    arrived = [[swap(sent, "feat", mask) for mask in peers] for sent in sents]
    total = ()
    for start, pair_sum, partners in zip(starts, sums, arrived):
        partners = partners if start else []
        (active,) = call(
            functools.partial(gelu_kernel, start, hidden_width, block_width, full_width, len(peers)),
            [((half, width), bf16)],
            [in_vmem] * (3 + len(peers) + len(partners)),
            [pltpu.VMEM((1 + len(peers), half, side), f32)],
        )(up_bias[None, :], pair_sum, sents[0], *arrived[0], *partners)
        last = start == starts[-1]
        total = call(
            functools.partial(down_kernel, start, last),
            [((half, block_width), f32), ((half, block_width), bf16)]
            if last
            else [((2 * half, block_width), f32)],
            [in_vmem] * (3 + len(total)),
            [pltpu.VMEM((2 * half, width), bf16)],
            flops=4 * half * width * block_width,
        )(active, swap(active, "feat", 1), down_weight, *total)
    near_sum, far_sum = total

    near_sum = near_sum + swap(far_sum, "tok", 1)
    blocks = near_sum.reshape(tok_size // 2, tok_rows, block_width)
    summed = blocks[0]
    sent = blocks.astype(bf16)
    for part in [swap(sent[mask // 2], "tok", mask) for mask in masks]:
        summed = summed + part

    positions = jnp.arange(tok_rows, dtype=jnp.int32)
    valid_rows = ((positions // FRAME_TOK < frame_counts) & (patch_mask == 1)).astype(f32)
    return (valid_rows[:, None] * (summed + down_bias[None, :])).astype(bf16)


def solution(mesh):
    in_specs = (
        P("tok", "feat"),
        P("tok"),
        P("tok"),
        P("feat"),
        P("feat", "tok"),
        P("tok"),
        P("tok", "feat"),
        P("feat"),
    )
    out_specs = P("tok", "feat")
    return jax.shard_map(
        per_device, mesh=mesh, in_specs=in_specs, out_specs=out_specs, check_vma=False
    )
```

```python
import functools

import jax
import jax.numpy as jnp
from jax import lax
from jax.experimental import pallas as pl
from jax.experimental.pallas import tpu as pltpu
from jax.sharding import PartitionSpec as P

FRAME_TOK = 4
LANES = 128
MIB = 2**20
PARTS = 2

epsilon = 1e-06

in_vmem = pl.BlockSpec(memory_space=pltpu.VMEM)
in_hbm = pl.BlockSpec(memory_space=pltpu.HBM)


def swap(block, axis, mask):
    size = lax.axis_size(axis)
    return lax.ppermute(block, axis, [(i, i ^ mask) for i in range(size)])


def is_first_core():
    return lax.rem(lax.axis_index("feat"), 2) == 0


def tile_of(width):
    return next((t for t in (512, 384, 256, 128) if width % t == 0), width)


def call(kernel, outs, in_specs, scratch=(), flops=0, limit=4):
    outs = [jax.ShapeDtypeStruct(shape, dtype) for shape, dtype in outs]
    return pl.pallas_call(
        kernel,
        out_shape=outs,
        in_specs=in_specs,
        out_specs=[in_vmem] * len(outs),
        scratch_shapes=list(scratch),
        compiler_params=pltpu.CompilerParams(vmem_limit_bytes=limit * MIB),
        cost_estimate=pl.CostEstimate(
            flops=flops, bytes_accessed=sum(o.size * 4 for o in outs), transcendentals=0
        ),
    )


def pieces(column):
    high = column.astype(jnp.bfloat16).astype(jnp.float32)
    middle = (column - high).astype(jnp.bfloat16).astype(jnp.float32)
    return high, middle, column - high - middle


def pack(sums, squares):
    lane = lax.broadcasted_iota(jnp.int32, (sums.shape[0], LANES), 1)
    packed = jnp.zeros((sums.shape[0], LANES), jnp.float32)
    for at, piece in enumerate(pieces(sums) + pieces(squares)):
        packed = jnp.where(lane == at, piece, packed)
    return packed.astype(jnp.bfloat16)


def unpack(packed):
    packed = packed.astype(jnp.float32)
    column = [packed[:, at:at + 1] for at in range(6)]
    return column[0] + column[1] + column[2], column[3] + column[4] + column[5]


def pack_row(row_of, width, scratch, out_ref):
    count = width // LANES
    scratch[...] = jnp.zeros_like(scratch)
    for at in range(count):
        piece = row_of(at * LANES)
        high = piece.astype(jnp.bfloat16).astype(jnp.float32)
        for place, value in ((at, high), (count + at, piece - high)):
            group, line = divmod(place, scratch.shape[0])
            scratch[line:line + 1, group * LANES:(group + 1) * LANES] = value
    out_ref[...] = scratch[...].astype(jnp.bfloat16)


def unpack_row(packed, start, stop, width):
    count = width // LANES
    pieces = []
    for at in range(start // LANES, stop // LANES):
        piece = 0
        for place in (at, count + at):
            group, line = divmod(place, packed.shape[0])
            piece = piece + packed[line:line + 1, group * LANES:(group + 1) * LANES]
        pieces.append(piece)
    return jnp.concatenate(pieces, axis=1)


def load_kernel(start, weight_ref, out_ref, sem):
    copy = pltpu.make_async_copy(weight_ref.at[:, pl.ds(start, out_ref.shape[1])], out_ref, sem)
    copy.start()
    copy.wait()


def load_last_kernel(start, gain_ref, *refs):
    weight_ref, out_ref, row_ref, packed_ref, scratch, sem = refs[-6:]
    width = out_ref.shape[1]
    copy = pltpu.make_async_copy(weight_ref.at[:, pl.ds(start, width)], out_ref, sem)
    copy.start()
    gain = gain_ref[...][None, :]
    high = gain.astype(jnp.bfloat16).astype(jnp.float32)
    row = lax.broadcasted_iota(jnp.int32, (16, gain.shape[1]), 0)
    rows = jnp.where(row == 0, high, jnp.where(row == 1, gain - high, 0.0)).astype(jnp.bfloat16)
    tile = tile_of(width)
    for part, loaded in enumerate(refs[:-6] + (out_ref,)):
        if loaded is out_ref:
            copy.wait()
        for at in range(0, width, tile):
            product = jnp.dot(rows, loaded[:, at:at + tile], preferred_element_type=jnp.float32)
            row_ref[:, part * width + at:part * width + at + tile] = product[0:1] + product[1:2]
    pack_row(lambda at: row_ref[:, at:at + LANES], row_ref.shape[1], scratch, packed_ref)


def up_kernel(near_ref, far_ref, gain_ref, packed_ref, weight_ref, rows_ref, own_ref, kept_ref, given_ref):
    half, block_width = near_ref.shape
    width = kept_ref.shape[1]
    first = is_first_core()
    near, far = near_ref[...].astype(jnp.float32), far_ref[...].astype(jnp.float32)
    for at, values in enumerate((jnp.where(first, near, far), jnp.where(first, far, near))):
        sums = jnp.sum(values, axis=1, keepdims=True)
        squares = jnp.sum(values * values, axis=1, keepdims=True)
        centred = (values - sums / block_width) * gain_ref[...][None, :]
        rows_ref[at * half:(at + 1) * half] = centred.astype(jnp.bfloat16)
        packed = pack(sums, squares)
        if at == 0:
            own_ref[...] = packed
        else:
            given_ref[:, width:width + LANES] = packed
    given_ref[:, width + LANES:] = packed_ref[...]
    up_products(rows_ref, weight_ref, kept_ref, given_ref)


def up_products(rows_ref, weight_ref, kept_ref, given_ref):
    half, width = kept_ref.shape
    tile = tile_of(width)
    for at in range(0, width, tile):
        product = jnp.dot(
            rows_ref[...], weight_ref[:, at:at + tile], preferred_element_type=jnp.float32
        )
        kept_ref[:, at:at + tile] = product[:half]
        given_ref[:, at:at + tile] = product[half:].astype(jnp.bfloat16)


def pair_kernel(start, full, block_width, kept_ref, own_ref, gain_ref, packed_ref, other_ref, sum_ref, sent_ref, scratch):
    width = kept_ref.shape[1]
    side = other_ref if start == 0 else packed_ref
    sums, squares = unpack(own_ref[...])
    other_sums, other_squares = unpack(side[:, width:width + LANES])
    shift = (sums - other_sums) / (2 * block_width)
    scratch[...] = side[:, width + LANES:].astype(jnp.float32)
    tile = tile_of(width)
    for at in range(0, width, tile):
        cut, there = slice(at, at + tile), slice(start + at, start + at + tile)
        gains = gain_ref[:, there] - unpack_row(scratch, there.start, there.stop, full)
        total = kept_ref[:, cut] + other_ref[:, cut].astype(jnp.float32) + shift * gains
        sum_ref[:, cut] = total
        sent_ref[:, cut] = total.astype(jnp.bfloat16)
    if start == 0:
        sent_ref[:, width:width + LANES] = pack(sums + other_sums, squares + other_squares)
        rows = [gain_ref[:, at:at + LANES] + unpack_row(scratch, at, at + LANES, full) for at in range(0, full, LANES)]
        pack_row(lambda at: rows[at // LANES], full, scratch, sent_ref.at[:, width + LANES:])


def gelu_kernel(start, full, block_width, full_width, peers, bias_ref, sum_ref, *refs):
    out_ref, scratch = refs[-2:]
    packed, others = refs[:peers + 1], refs[peers + 1:-2] or refs[1:peers + 1]
    width = sum_ref.shape[1]
    stats = [unpack(ref[:, width:width + LANES]) for ref in packed]
    row_mean = sum(s[0] for s in stats) / full_width
    spread = sum(s[1] for s in stats) / full_width - row_mean * row_mean
    scale = lax.rsqrt(spread + epsilon)
    shifts = [s[0] / (2 * block_width) - row_mean for s in stats]
    for at, ref in enumerate(packed):
        scratch[at] = ref[:, width + LANES:].astype(jnp.float32)
    tile = tile_of(width)
    for at in range(0, width, tile):
        cut, there = slice(at, at + tile), slice(start + at, start + at + tile)
        total = sum_ref[:, cut]
        for other in others:
            total = total + other[:, cut].astype(jnp.float32)
        for at, shift in enumerate(shifts):
            total = total + shift * unpack_row(scratch.at[at], there.start, there.stop, full)
        active = jax.nn.gelu(total * scale + bias_ref[:, there], approximate=True)
        out_ref[:, cut] = active.astype(jnp.bfloat16)


def down_kernel(start, last, kept_ref, given_ref, weight_ref, *refs):
    half, depth = kept_ref.shape
    rows_ref = refs[-1]
    rows_ref[:half] = kept_ref[...]
    rows_ref[half:] = given_ref[...]
    first = is_first_core()
    width = weight_ref.shape[1]
    tile = tile_of(width)
    for at in range(0, width, tile):
        cut = slice(at, at + tile)
        product = jnp.dot(
            rows_ref[...], weight_ref[start:start + depth, cut], preferred_element_type=jnp.float32
        )
        if start:
            product = product + refs[0][:, cut]
        if last:
            kept, given = product[:half], product[half:]
            refs[-3][:, cut] = jnp.where(first, kept, given)
            refs[-2][:, cut] = jnp.where(first, given, kept).astype(jnp.bfloat16)
        else:
            refs[-2][:, cut] = product


def per_device(
    patches, frame_counts, patch_mask, norm_gain, up_weight, up_bias, down_weight, down_bias
):
    tok_rows, block_width = patches.shape
    hidden_width = up_weight.shape[1]
    tok_size = lax.axis_size("tok")
    feat_size = lax.axis_size("feat")
    full_width = block_width * feat_size
    f32, bf16 = jnp.float32, jnp.bfloat16

    parts = PARTS if hidden_width % (PARTS * LANES) == 0 else 1
    width = hidden_width // parts
    starts = range(0, hidden_width, width)

    masks = range(2, tok_size, 2)
    peers = range(2, feat_size, 2)
    half = tok_rows * tok_size // 2
    side = LANES * -(-2 * hidden_width // (LANES * half))
    extra = [LANES + side if start == 0 else 0 for start in starts]
    copied = pltpu.SemaphoreType.DMA
    loaded = [
        call(
            functools.partial(load_kernel, start),
            [((block_width, width), bf16)],
            [in_hbm],
            [copied],
            limit=46,
        )(up_weight)[0]
        for start in starts[:-1]
    ]
    order = [0] + list(reversed(masks))
    near = jnp.concatenate([patches] + [swap(patches, "tok", mask) for mask in order[1:]])
    near, loaded, norm_gain = lax.optimization_barrier((near, loaded, norm_gain))
    far = swap(near, "tok", 1)
    last, gain_row, gain_packed = call(
        functools.partial(load_last_kernel, starts[-1]),
        [((block_width, width), bf16), ((1, hidden_width), f32), ((half, side), bf16)],
        [in_vmem] * parts + [in_hbm],
        [pltpu.VMEM((half, side), f32), copied],
        flops=32 * up_weight.size,
        limit=40,
    )(norm_gain, *loaded, up_weight)
    loaded = loaded + [last]

    kepts, givens = [], []
    for start, more, weight in zip(starts, extra, loaded):
        outs = [((half, width), f32), ((half, width + more), bf16)]
        flops = 4 * half * block_width * width
        if start == 0:
            rows, own, kept, given = call(
                up_kernel,
                [((2 * half, block_width), bf16), ((half, LANES), bf16)] + outs,
                [in_vmem] * 5,
                flops=flops,
            )(near, far, norm_gain, gain_packed, weight)
        else:
            kept, given = call(
                up_products, outs, [in_vmem] * 2, flops=flops
            )(rows, weight)
        kepts.append(kept)
        givens.append(given)
    others = [swap(given, "feat", 1) for given in givens]
    sums, sents = [], []
    for start, more, kept, other in zip(starts, extra, kepts, others):
        pair_sum, sent = call(
            functools.partial(pair_kernel, start, hidden_width, block_width),
            [((half, width), f32), ((half, width + more), bf16)],
            [in_vmem] * 5,
            [pltpu.VMEM((half, side), f32)],
        )(kept, own, gain_row, others[0], other)
        sums.append(pair_sum)
        sents.append(sent)
    arrived = [[swap(sent, "feat", mask) for mask in peers] for sent in sents]
    total = ()
    for start, pair_sum, partners in zip(starts, sums, arrived):
        partners = partners if start else []
        (active,) = call(
            functools.partial(gelu_kernel, start, hidden_width, block_width, full_width, len(peers)),
            [((half, width), bf16)],
            [in_vmem] * (3 + len(peers) + len(partners)),
            [pltpu.VMEM((1 + len(peers), half, side), f32)],
        )(up_bias[None, :], pair_sum, sents[0], *arrived[0], *partners)
        last = start == starts[-1]
        total = call(
            functools.partial(down_kernel, start, last),
            [((half, block_width), f32), ((half, block_width), bf16)]
            if last
            else [((2 * half, block_width), f32)],
            [in_vmem] * (3 + len(total)),
            [pltpu.VMEM((2 * half, width), bf16)],
            flops=4 * half * width * block_width,
        )(active, swap(active, "feat", 1), down_weight, *total)
    near_sum, far_sum = total

    near_sum = near_sum + swap(far_sum, "tok", 1)
    blocks = near_sum.reshape(tok_size // 2, tok_rows, block_width)
    summed = blocks[0]
    sent = blocks.astype(bf16)
    for part in [swap(sent[order.index(mask)], "tok", mask) for mask in reversed(masks)]:
        summed = summed + part

    positions = jnp.arange(tok_rows, dtype=jnp.int32)
    valid_rows = ((positions // FRAME_TOK < frame_counts) & (patch_mask == 1)).astype(f32)
    return (valid_rows[:, None] * (summed + down_bias[None, :])).astype(bf16)


def solution(mesh):
    in_specs = (
        P("tok", "feat"),
        P("tok"),
        P("tok"),
        P("feat"),
        P("feat", "tok"),
        P("tok"),
        P("tok", "feat"),
        P("feat"),
    )
    out_specs = P("tok", "feat")
    return jax.shard_map(
        per_device, mesh=mesh, in_specs=in_specs, out_specs=out_specs, check_vma=False
    )
```

```python
import functools

import jax
import jax.numpy as jnp
from jax import lax
from jax.experimental import pallas as pl
from jax.experimental.pallas import tpu as pltpu
from jax.sharding import PartitionSpec as P

FRAME_TOK = 4
LANES = 128
MIB = 2**20
PARTS = 2

epsilon = 1e-06

in_vmem = pl.BlockSpec(memory_space=pltpu.VMEM)
in_hbm = pl.BlockSpec(memory_space=pltpu.HBM)


def swap(block, axis, mask):
    size = lax.axis_size(axis)
    return lax.ppermute(block, axis, [(i, i ^ mask) for i in range(size)])


def is_first_core():
    return lax.rem(lax.axis_index("feat"), 2) == 0


def tile_of(width):
    return next((t for t in (512, 384, 256, 128) if width % t == 0), width)


def call(kernel, outs, in_specs, scratch=(), flops=0, limit=4):
    outs = [jax.ShapeDtypeStruct(shape, dtype) for shape, dtype in outs]
    return pl.pallas_call(
        kernel,
        out_shape=outs,
        in_specs=in_specs,
        out_specs=[in_vmem] * len(outs),
        scratch_shapes=list(scratch),
        compiler_params=pltpu.CompilerParams(vmem_limit_bytes=limit * MIB),
        cost_estimate=pl.CostEstimate(
            flops=8 * flops, bytes_accessed=0, transcendentals=0
        ),
    )


def pieces(column):
    high = column.astype(jnp.bfloat16).astype(jnp.float32)
    middle = (column - high).astype(jnp.bfloat16).astype(jnp.float32)
    return high, middle, column - high - middle


def pack(sums, squares):
    lane = lax.broadcasted_iota(jnp.int32, (sums.shape[0], LANES), 1)
    packed = jnp.zeros((sums.shape[0], LANES), jnp.float32)
    for at, piece in enumerate(pieces(sums) + pieces(squares)):
        packed = jnp.where(lane == at, piece, packed)
    return packed.astype(jnp.bfloat16)


def unpack(packed):
    packed = packed.astype(jnp.float32)
    column = [packed[:, at:at + 1] for at in range(6)]
    return column[0] + column[1] + column[2], column[3] + column[4] + column[5]


def pack_row(row_of, width, scratch, out_ref):
    count = width // LANES
    scratch[...] = jnp.zeros_like(scratch)
    for at in range(count):
        piece = row_of(at * LANES)
        high = piece.astype(jnp.bfloat16).astype(jnp.float32)
        for place, value in ((at, high), (count + at, piece - high)):
            group, line = divmod(place, scratch.shape[0])
            scratch[line:line + 1, group * LANES:(group + 1) * LANES] = value
    out_ref[...] = scratch[...].astype(jnp.bfloat16)


def unpack_row(packed, start, stop, width):
    count = width // LANES
    pieces = []
    for at in range(start // LANES, stop // LANES):
        piece = 0
        for place in (at, count + at):
            group, line = divmod(place, packed.shape[0])
            piece = piece + packed[line:line + 1, group * LANES:(group + 1) * LANES]
        pieces.append(piece)
    return jnp.concatenate(pieces, axis=1)


def load_kernel(start, weight_ref, out_ref, sem):
    copy = pltpu.make_async_copy(weight_ref.at[:, pl.ds(start, out_ref.shape[1])], out_ref, sem)
    copy.start()
    copy.wait()


def load_last_kernel(start, gain_ref, *refs):
    weight_ref, out_ref, row_ref, packed_ref, scratch, sems = refs[-6:]
    width = out_ref.shape[1]
    tile = tile_of(width)
    tiles = range(0, width, tile)
    copies = [
        pltpu.make_async_copy(
            weight_ref.at[:, pl.ds(start + at, tile)], out_ref.at[:, pl.ds(at, tile)], sems.at[at // tile]
        )
        for at in tiles
    ]
    for copy in copies:
        copy.start()
    gain = gain_ref[...][None, :]
    high = gain.astype(jnp.bfloat16).astype(jnp.float32)
    row = lax.broadcasted_iota(jnp.int32, (16, gain.shape[1]), 0)
    rows = jnp.where(row == 0, high, jnp.where(row == 1, gain - high, 0.0)).astype(jnp.bfloat16)
    for part, loaded in enumerate(refs[:-6] + (out_ref,)):
        for at, copy in zip(tiles, copies):
            if loaded is out_ref:
                copy.wait()
            product = jnp.dot(rows, loaded[:, at:at + tile], preferred_element_type=jnp.float32)
            row_ref[:, part * width + at:part * width + at + tile] = product[0:1] + product[1:2]
    pack_row(lambda at: row_ref[:, at:at + LANES], row_ref.shape[1], scratch, packed_ref)


def up_kernel(near_ref, far_ref, gain_ref, packed_ref, weight_ref, rows_ref, own_ref, kept_ref, given_ref):
    half, block_width = near_ref.shape
    width = kept_ref.shape[1]
    first = is_first_core()
    near, far = near_ref[...].astype(jnp.float32), far_ref[...].astype(jnp.float32)
    for at, values in enumerate((jnp.where(first, near, far), jnp.where(first, far, near))):
        sums = jnp.sum(values, axis=1, keepdims=True)
        squares = jnp.sum(values * values, axis=1, keepdims=True)
        centred = (values - sums / block_width) * gain_ref[...][None, :]
        rows_ref[at * half:(at + 1) * half] = centred.astype(jnp.bfloat16)
        packed = pack(sums, squares)
        if at == 0:
            own_ref[...] = packed
        else:
            given_ref[:, width:width + LANES] = packed
    given_ref[:, width + LANES:] = packed_ref[...]
    up_products(rows_ref, weight_ref, kept_ref, given_ref)


def up_products(rows_ref, weight_ref, kept_ref, given_ref):
    half, width = kept_ref.shape
    tile = tile_of(width)
    for at in range(0, width, tile):
        product = jnp.dot(
            rows_ref[...], weight_ref[:, at:at + tile], preferred_element_type=jnp.float32
        )
        kept_ref[:, at:at + tile] = product[:half]
        given_ref[:, at:at + tile] = product[half:].astype(jnp.bfloat16)


def pair_kernel(start, full, block_width, kept_ref, own_ref, gain_ref, packed_ref, other_ref, sum_ref, sent_ref, scratch):
    width = kept_ref.shape[1]
    side = other_ref if start == 0 else packed_ref
    sums, squares = unpack(own_ref[...])
    other_sums, other_squares = unpack(side[:, width:width + LANES])
    shift = (sums - other_sums) / (2 * block_width)
    scratch[...] = side[:, width + LANES:].astype(jnp.float32)
    tile = tile_of(width)
    for at in range(0, width, tile):
        cut, there = slice(at, at + tile), slice(start + at, start + at + tile)
        gains = gain_ref[:, there] - unpack_row(scratch, there.start, there.stop, full)
        total = kept_ref[:, cut] + other_ref[:, cut].astype(jnp.float32) + shift * gains
        sum_ref[:, cut] = total
        sent_ref[:, cut] = total.astype(jnp.bfloat16)
    if start == 0:
        sent_ref[:, width:width + LANES] = pack(sums + other_sums, squares + other_squares)
        rows = [gain_ref[:, at:at + LANES] + unpack_row(scratch, at, at + LANES, full) for at in range(0, full, LANES)]
        pack_row(lambda at: rows[at // LANES], full, scratch, sent_ref.at[:, width + LANES:])


def gelu_kernel(start, full, block_width, full_width, peers, bias_ref, sum_ref, *refs):
    out_ref, scratch = refs[-2:]
    packed, others = refs[:peers + 1], refs[peers + 1:-2] or refs[1:peers + 1]
    width = sum_ref.shape[1]
    stats = [unpack(ref[:, width:width + LANES]) for ref in packed]
    row_mean = sum(s[0] for s in stats) / full_width
    spread = sum(s[1] for s in stats) / full_width - row_mean * row_mean
    scale = lax.rsqrt(spread + epsilon)
    shifts = [s[0] / (2 * block_width) - row_mean for s in stats]
    for at, ref in enumerate(packed):
        scratch[at] = ref[:, width + LANES:].astype(jnp.float32)
    tile = tile_of(width)
    for at in range(0, width, tile):
        cut, there = slice(at, at + tile), slice(start + at, start + at + tile)
        total = sum_ref[:, cut]
        for other in others:
            total = total + other[:, cut].astype(jnp.float32)
        for at, shift in enumerate(shifts):
            total = total + shift * unpack_row(scratch.at[at], there.start, there.stop, full)
        active = jax.nn.gelu(total * scale + bias_ref[:, there], approximate=True)
        out_ref[:, cut] = active.astype(jnp.bfloat16)


def down_kernel(start, last, kept_ref, given_ref, weight_ref, *refs):
    half, depth = kept_ref.shape
    rows_ref = refs[-1]
    rows_ref[:half] = kept_ref[...]
    rows_ref[half:] = given_ref[...]
    first = is_first_core()
    width = weight_ref.shape[1]
    tile = tile_of(width)
    for at in range(0, width, tile):
        cut = slice(at, at + tile)
        product = jnp.dot(
            rows_ref[...], weight_ref[start:start + depth, cut], preferred_element_type=jnp.float32
        )
        if start:
            product = product + refs[0][:, cut]
        if last:
            kept, given = product[:half], product[half:]
            refs[-3][:, cut] = jnp.where(first, kept, given)
            refs[-2][:, cut] = jnp.where(first, given, kept).astype(jnp.bfloat16)
        else:
            refs[-2][:, cut] = product


def per_device(
    patches, frame_counts, patch_mask, norm_gain, up_weight, up_bias, down_weight, down_bias
):
    tok_rows, block_width = patches.shape
    hidden_width = up_weight.shape[1]
    tok_size = lax.axis_size("tok")
    feat_size = lax.axis_size("feat")
    full_width = block_width * feat_size
    f32, bf16 = jnp.float32, jnp.bfloat16

    parts = PARTS if hidden_width % (PARTS * LANES) == 0 else 1
    width = hidden_width // parts
    starts = range(0, hidden_width, width)

    masks = range(2, tok_size, 2)
    peers = range(2, feat_size, 2)
    half = tok_rows * tok_size // 2
    side = LANES * -(-2 * hidden_width // (LANES * half))
    extra = [LANES + side if start == 0 else 0 for start in starts]
    copied = pltpu.SemaphoreType.DMA
    loaded = [
        call(
            functools.partial(load_kernel, start),
            [((block_width, width), bf16)],
            [in_hbm],
            [copied],
            limit=46,
        )(up_weight)[0]
        for start in starts[:-1]
    ]
    order = [0] + list(reversed(masks))
    near = jnp.concatenate([patches] + [swap(patches, "tok", mask) for mask in order[1:]])
    near, loaded, norm_gain = lax.optimization_barrier((near, loaded, norm_gain))
    far = swap(near, "tok", 1)
    last, gain_row, gain_packed = call(
        functools.partial(load_last_kernel, starts[-1]),
        [((block_width, width), bf16), ((1, hidden_width), f32), ((half, side), bf16)],
        [in_vmem] * parts + [in_hbm],
        [pltpu.VMEM((half, side), f32), copied((width // tile_of(width),))],
        flops=32 * up_weight.size,
        limit=40,
    )(norm_gain, *loaded, up_weight)
    loaded = loaded + [last]

    kepts, givens = [], []
    for start, more, weight in zip(starts, extra, loaded):
        outs = [((half, width), f32), ((half, width + more), bf16)]
        flops = 4 * half * block_width * width
        if start == 0:
            rows, own, kept, given = call(
                up_kernel,
                [((2 * half, block_width), bf16), ((half, LANES), bf16)] + outs,
                [in_vmem] * 5,
                flops=flops,
            )(near, far, norm_gain, gain_packed, weight)
        else:
            kept, given = call(
                up_products, outs, [in_vmem] * 2, flops=flops
            )(rows, weight)
        kepts.append(kept)
        givens.append(given)
    others = [swap(given, "feat", 1) for given in givens]
    sums, sents = [], []
    for start, more, kept, other in zip(starts, extra, kepts, others):
        pair_sum, sent = call(
            functools.partial(pair_kernel, start, hidden_width, block_width),
            [((half, width), f32), ((half, width + more), bf16)],
            [in_vmem] * 5,
            [pltpu.VMEM((half, side), f32)],
        )(kept, own, gain_row, others[0], other)
        sums.append(pair_sum)
        sents.append(sent)
    arrived = [[swap(sent, "feat", mask) for mask in peers] for sent in sents]
    total = ()
    for start, pair_sum, partners in zip(starts, sums, arrived):
        partners = partners if start else []
        (active,) = call(
            functools.partial(gelu_kernel, start, hidden_width, block_width, full_width, len(peers)),
            [((half, width), bf16)],
            [in_vmem] * (3 + len(peers) + len(partners)),
            [pltpu.VMEM((1 + len(peers), half, side), f32)],
        )(up_bias[None, :], pair_sum, sents[0], *arrived[0], *partners)
        last = start == starts[-1]
        total = call(
            functools.partial(down_kernel, start, last),
            [((half, block_width), f32), ((half, block_width), bf16)]
            if last
            else [((2 * half, block_width), f32)],
            [in_vmem] * (3 + len(total)),
            [pltpu.VMEM((2 * half, width), bf16)],
            flops=4 * half * width * block_width,
        )(active, swap(active, "feat", 1), down_weight, *total)
    near_sum, far_sum = total

    def rows_of(array, masks):
        at = [order.index(mask) * tok_rows for mask in masks]
        return jnp.concatenate([array[start:start + tok_rows] for start in at])

    first, second = order[1:1 + len(order) // 2], order[1 + len(order) // 2:] + [0]
    summed = 0
    for group in (first, second):
        total = rows_of(near_sum, group) + swap(rows_of(far_sum, group), "tok", 1)
        for at, mask in enumerate(group):
            block = total[at * tok_rows:(at + 1) * tok_rows]
            summed = summed + (swap(block.astype(bf16), "tok", mask) if mask else block)

    positions = jnp.arange(tok_rows, dtype=jnp.int32)
    valid_rows = ((positions // FRAME_TOK < frame_counts) & (patch_mask == 1)).astype(f32)
    return (valid_rows[:, None] * (summed + down_bias[None, :])).astype(bf16)


def solution(mesh):
    in_specs = (
        P("tok", "feat"),
        P("tok"),
        P("tok"),
        P("feat"),
        P("feat", "tok"),
        P("tok"),
        P("tok", "feat"),
        P("feat"),
    )
    out_specs = P("tok", "feat")
    return jax.shard_map(
        per_device, mesh=mesh, in_specs=in_specs, out_specs=out_specs, check_vma=False
    )
```

```python
import functools

import jax
import jax.numpy as jnp
from jax import lax
from jax.experimental import pallas as pl
from jax.experimental.pallas import tpu as pltpu
from jax.sharding import PartitionSpec as P

FRAME_TOK = 4
LANES = 128
MIB = 2**20
PARTS = 3

epsilon = 1e-06

in_vmem = pl.BlockSpec(memory_space=pltpu.VMEM)
in_hbm = pl.BlockSpec(memory_space=pltpu.HBM)


def swap(block, axis, mask):
    size = lax.axis_size(axis)
    return lax.ppermute(block, axis, [(i, i ^ mask) for i in range(size)])


def is_first_core():
    return lax.rem(lax.axis_index("feat"), 2) == 0


def tile_of(width):
    return next((t for t in (512, 384, 256, 128) if width % t == 0), width)


def call(kernel, outs, in_specs, scratch=(), flops=0, limit=4):
    outs = [jax.ShapeDtypeStruct(shape, dtype) for shape, dtype in outs]
    return pl.pallas_call(
        kernel,
        out_shape=outs,
        in_specs=in_specs,
        out_specs=[in_vmem] * len(outs),
        scratch_shapes=list(scratch),
        compiler_params=pltpu.CompilerParams(vmem_limit_bytes=limit * MIB),
        cost_estimate=pl.CostEstimate(
            flops=8 * flops, bytes_accessed=0, transcendentals=0
        ),
    )


def pieces(column):
    high = column.astype(jnp.bfloat16).astype(jnp.float32)
    middle = (column - high).astype(jnp.bfloat16).astype(jnp.float32)
    return high, middle, column - high - middle


def pack(sums, squares):
    lane = lax.broadcasted_iota(jnp.int32, (sums.shape[0], LANES), 1)
    packed = jnp.zeros((sums.shape[0], LANES), jnp.float32)
    for at, piece in enumerate(pieces(sums) + pieces(squares)):
        packed = jnp.where(lane == at, piece, packed)
    return packed.astype(jnp.bfloat16)


def unpack(packed):
    packed = packed.astype(jnp.float32)
    column = [packed[:, at:at + 1] for at in range(6)]
    return column[0] + column[1] + column[2], column[3] + column[4] + column[5]


def pack_row(row_of, width, scratch, out_ref):
    count = width // LANES
    scratch[...] = jnp.zeros_like(scratch)
    for at in range(count):
        piece = row_of(at * LANES)
        high = piece.astype(jnp.bfloat16).astype(jnp.float32)
        for place, value in ((at, high), (count + at, piece - high)):
            group, line = divmod(place, scratch.shape[0])
            scratch[line:line + 1, group * LANES:(group + 1) * LANES] = value
    out_ref[...] = scratch[...].astype(jnp.bfloat16)


def unpack_row(packed, start, stop, width):
    count = width // LANES
    pieces = []
    for at in range(start // LANES, stop // LANES):
        piece = 0
        for place in (at, count + at):
            group, line = divmod(place, packed.shape[0])
            piece = piece + packed[line:line + 1, group * LANES:(group + 1) * LANES]
        pieces.append(piece)
    return jnp.concatenate(pieces, axis=1)


def load_kernel(start, weight_ref, out_ref, sem):
    copy = pltpu.make_async_copy(weight_ref.at[:, pl.ds(start, out_ref.shape[1])], out_ref, sem)
    copy.start()
    copy.wait()


def load_rest_kernel(gain_ref, first_ref, weight_ref, *refs):
    outs, (row_ref, packed_ref, scratch, sems) = refs[:-4], refs[-4:]
    width = first_ref.shape[1]
    tile = tile_of(width)
    tiles = range(0, width, tile)
    copies = {}
    for part, out_ref in enumerate(outs, 1):
        for at in tiles:
            copy = pltpu.make_async_copy(
                weight_ref.at[:, pl.ds(part * width + at, tile)],
                out_ref.at[:, pl.ds(at, tile)],
                sems.at[len(copies)],
            )
            copy.start()
            copies[part, at] = copy
    gain = gain_ref[...][None, :]
    high = gain.astype(jnp.bfloat16).astype(jnp.float32)
    row = lax.broadcasted_iota(jnp.int32, (16, gain.shape[1]), 0)
    rows = jnp.where(row == 0, high, jnp.where(row == 1, gain - high, 0.0)).astype(jnp.bfloat16)
    for part, loaded in enumerate((first_ref,) + outs):
        for at in tiles:
            if part:
                copies[part, at].wait()
            product = jnp.dot(rows, loaded[:, at:at + tile], preferred_element_type=jnp.float32)
            row_ref[:, part * width + at:part * width + at + tile] = product[0:1] + product[1:2]
    pack_row(lambda at: row_ref[:, at:at + LANES], row_ref.shape[1], scratch, packed_ref)


def up_kernel(near_ref, far_ref, gain_ref, packed_ref, weight_ref, rows_ref, own_ref, kept_ref, given_ref):
    half, block_width = near_ref.shape
    width = kept_ref.shape[1]
    first = is_first_core()
    near, far = near_ref[...].astype(jnp.float32), far_ref[...].astype(jnp.float32)
    for at, values in enumerate((jnp.where(first, near, far), jnp.where(first, far, near))):
        sums = jnp.sum(values, axis=1, keepdims=True)
        squares = jnp.sum(values * values, axis=1, keepdims=True)
        centred = (values - sums / block_width) * gain_ref[...][None, :]
        rows_ref[at * half:(at + 1) * half] = centred.astype(jnp.bfloat16)
        packed = pack(sums, squares)
        if at == 0:
            own_ref[...] = packed
        else:
            given_ref[:, width:width + LANES] = packed
    given_ref[:, width + LANES:] = packed_ref[...]
    up_products(rows_ref, weight_ref, kept_ref, given_ref)


def up_products(rows_ref, weight_ref, kept_ref, given_ref):
    half, width = kept_ref.shape
    tile = tile_of(width)
    for at in range(0, width, tile):
        product = jnp.dot(
            rows_ref[...], weight_ref[:, at:at + tile], preferred_element_type=jnp.float32
        )
        kept_ref[:, at:at + tile] = product[:half]
        given_ref[:, at:at + tile] = product[half:].astype(jnp.bfloat16)


def pair_kernel(start, full, block_width, kept_ref, own_ref, gain_ref, packed_ref, other_ref, sum_ref, sent_ref, scratch):
    width = kept_ref.shape[1]
    side = other_ref if start == 0 else packed_ref
    sums, squares = unpack(own_ref[...])
    other_sums, other_squares = unpack(side[:, width:width + LANES])
    shift = (sums - other_sums) / (2 * block_width)
    scratch[...] = side[:, width + LANES:].astype(jnp.float32)
    tile = tile_of(width)
    for at in range(0, width, tile):
        cut, there = slice(at, at + tile), slice(start + at, start + at + tile)
        gains = gain_ref[:, there] - unpack_row(scratch, there.start, there.stop, full)
        total = kept_ref[:, cut] + other_ref[:, cut].astype(jnp.float32) + shift * gains
        sum_ref[:, cut] = total
        sent_ref[:, cut] = total.astype(jnp.bfloat16)
    if start == 0:
        sent_ref[:, width:width + LANES] = pack(sums + other_sums, squares + other_squares)
        rows = [gain_ref[:, at:at + LANES] + unpack_row(scratch, at, at + LANES, full) for at in range(0, full, LANES)]
        pack_row(lambda at: rows[at // LANES], full, scratch, sent_ref.at[:, width + LANES:])


def gelu_kernel(start, full, block_width, full_width, peers, bias_ref, sum_ref, *refs):
    out_ref, scratch = refs[-2:]
    packed, others = refs[:peers + 1], refs[peers + 1:-2] or refs[1:peers + 1]
    width = sum_ref.shape[1]
    stats = [unpack(ref[:, width:width + LANES]) for ref in packed]
    row_mean = sum(s[0] for s in stats) / full_width
    spread = sum(s[1] for s in stats) / full_width - row_mean * row_mean
    scale = lax.rsqrt(spread + epsilon)
    shifts = [s[0] / (2 * block_width) - row_mean for s in stats]
    for at, ref in enumerate(packed):
        scratch[at] = ref[:, width + LANES:].astype(jnp.float32)
    tile = tile_of(width)
    for at in range(0, width, tile):
        cut, there = slice(at, at + tile), slice(start + at, start + at + tile)
        total = sum_ref[:, cut]
        for other in others:
            total = total + other[:, cut].astype(jnp.float32)
        for at, shift in enumerate(shifts):
            total = total + shift * unpack_row(scratch.at[at], there.start, there.stop, full)
        active = jax.nn.gelu(total * scale + bias_ref[:, there], approximate=True)
        out_ref[:, cut] = active.astype(jnp.bfloat16)


def down_kernel(start, last, kept_ref, given_ref, weight_ref, *refs):
    half, depth = kept_ref.shape
    rows_ref = refs[-1]
    rows_ref[:half] = kept_ref[...]
    rows_ref[half:] = given_ref[...]
    first = is_first_core()
    width = weight_ref.shape[1]
    tile = tile_of(width)
    for at in range(0, width, tile):
        cut = slice(at, at + tile)
        product = jnp.dot(
            rows_ref[...], weight_ref[start:start + depth, cut], preferred_element_type=jnp.float32
        )
        if start:
            product = product + refs[0][:, cut]
        if last:
            kept, given = product[:half], product[half:]
            refs[-3][:, cut] = jnp.where(first, kept, given)
            refs[-2][:, cut] = jnp.where(first, given, kept).astype(jnp.bfloat16)
        else:
            refs[-2][:, cut] = product


def per_device(
    patches, frame_counts, patch_mask, norm_gain, up_weight, up_bias, down_weight, down_bias
):
    tok_rows, block_width = patches.shape
    hidden_width = up_weight.shape[1]
    tok_size = lax.axis_size("tok")
    feat_size = lax.axis_size("feat")
    full_width = block_width * feat_size
    f32, bf16 = jnp.float32, jnp.bfloat16

    parts = PARTS if hidden_width % (PARTS * LANES) == 0 else 1
    width = hidden_width // parts
    starts = range(0, hidden_width, width)

    masks = range(2, tok_size, 2)
    peers = range(2, feat_size, 2)
    half = tok_rows * tok_size // 2
    side = LANES * -(-2 * hidden_width // (LANES * half))
    extra = [LANES + side if start == 0 else 0 for start in starts]
    copied = pltpu.SemaphoreType.DMA
    (loaded,) = call(
        functools.partial(load_kernel, 0),
        [((block_width, width), bf16)],
        [in_hbm],
        [copied],
        limit=46,
    )(up_weight)
    order = [0] + list(reversed(masks))
    near = jnp.concatenate([patches] + [swap(patches, "tok", mask) for mask in order[1:]])
    near, loaded, norm_gain = lax.optimization_barrier((near, loaded, norm_gain))
    far = swap(near, "tok", 1)
    *rest, gain_row, gain_packed = call(
        load_rest_kernel,
        [((block_width, width), bf16)] * (parts - 1)
        + [((1, hidden_width), f32), ((half, side), bf16)],
        [in_vmem] * 2 + [in_hbm],
        [
            pltpu.VMEM((half, side), f32),
            copied(((parts - 1) * (width // tile_of(width)) or 1,)),
        ],
        flops=32 * up_weight.size,
        limit=40,
    )(norm_gain, loaded, up_weight)
    loaded = [loaded, *rest]

    kepts, givens = [], []
    for start, more, weight in zip(starts, extra, loaded):
        outs = [((half, width), f32), ((half, width + more), bf16)]
        flops = 4 * half * block_width * width
        if start == 0:
            rows, own, kept, given = call(
                up_kernel,
                [((2 * half, block_width), bf16), ((half, LANES), bf16)] + outs,
                [in_vmem] * 5,
                flops=flops,
            )(near, far, norm_gain, gain_packed, weight)
        else:
            kept, given = call(
                up_products, outs, [in_vmem] * 2, flops=flops
            )(rows, weight)
        kepts.append(kept)
        givens.append(given)
    others = [swap(given, "feat", 1) for given in givens]
    sums, sents = [], []
    for start, more, kept, other in zip(starts, extra, kepts, others):
        pair_sum, sent = call(
            functools.partial(pair_kernel, start, hidden_width, block_width),
            [((half, width), f32), ((half, width + more), bf16)],
            [in_vmem] * 5,
            [pltpu.VMEM((half, side), f32)],
        )(kept, own, gain_row, others[0], other)
        sums.append(pair_sum)
        sents.append(sent)
    arrived = [[swap(sent, "feat", mask) for mask in peers] for sent in sents]
    total = ()
    for start, pair_sum, partners in zip(starts, sums, arrived):
        partners = partners if start else []
        (active,) = call(
            functools.partial(gelu_kernel, start, hidden_width, block_width, full_width, len(peers)),
            [((half, width), bf16)],
            [in_vmem] * (3 + len(peers) + len(partners)),
            [pltpu.VMEM((1 + len(peers), half, side), f32)],
        )(up_bias[None, :], pair_sum, sents[0], *arrived[0], *partners)
        last = start == starts[-1]
        total = call(
            functools.partial(down_kernel, start, last),
            [((half, block_width), f32), ((half, block_width), bf16)]
            if last
            else [((2 * half, block_width), f32)],
            [in_vmem] * (3 + len(total)),
            [pltpu.VMEM((2 * half, width), bf16)],
            flops=4 * half * width * block_width,
        )(active, swap(active, "feat", 1), down_weight, *total)
    near_sum, far_sum = total

    def rows_of(array, masks):
        at = [order.index(mask) * tok_rows for mask in masks]
        return jnp.concatenate([array[start:start + tok_rows] for start in at])

    first, second = order[1:1 + len(order) // 2], order[1 + len(order) // 2:] + [0]
    summed = 0
    for group in (first, second):
        total = rows_of(near_sum, group) + swap(rows_of(far_sum, group), "tok", 1)
        for at, mask in enumerate(group):
            block = total[at * tok_rows:(at + 1) * tok_rows]
            summed = summed + (swap(block.astype(bf16), "tok", mask) if mask else block)

    positions = jnp.arange(tok_rows, dtype=jnp.int32)
    valid_rows = ((positions // FRAME_TOK < frame_counts) & (patch_mask == 1)).astype(f32)
    return (valid_rows[:, None] * (summed + down_bias[None, :])).astype(bf16)


def solution(mesh):
    in_specs = (
        P("tok", "feat"),
        P("tok"),
        P("tok"),
        P("feat"),
        P("feat", "tok"),
        P("tok"),
        P("tok", "feat"),
        P("feat"),
    )
    out_specs = P("tok", "feat")
    return jax.shard_map(
        per_device, mesh=mesh, in_specs=in_specs, out_specs=out_specs, check_vma=False
    )
```

```python
import functools

import jax
import jax.numpy as jnp
from jax import lax
from jax.experimental import pallas as pl
from jax.experimental.pallas import tpu as pltpu
from jax.sharding import PartitionSpec as P

FRAME_TOK = 4
LANES = 128
MIB = 2**20
PARTS = 3

epsilon = 1e-06

in_vmem = pl.BlockSpec(memory_space=pltpu.VMEM)
in_hbm = pl.BlockSpec(memory_space=pltpu.HBM)


def swap(block, axis, mask):
    size = lax.axis_size(axis)
    return lax.ppermute(block, axis, [(i, i ^ mask) for i in range(size)])


def is_first_core():
    return lax.rem(lax.axis_index("feat"), 2) == 0


def tile_of(width):
    return next((t for t in (512, 384, 256, 128) if width % t == 0), width)


def call(kernel, outs, in_specs, scratch=(), flops=0, limit=4):
    outs = [jax.ShapeDtypeStruct(shape, dtype) for shape, dtype in outs]
    return pl.pallas_call(
        kernel,
        out_shape=outs,
        in_specs=in_specs,
        out_specs=[in_vmem] * len(outs),
        scratch_shapes=list(scratch),
        compiler_params=pltpu.CompilerParams(vmem_limit_bytes=limit * MIB),
        cost_estimate=pl.CostEstimate(
            flops=8 * flops, bytes_accessed=0, transcendentals=0
        ),
    )


def pieces(column):
    high = column.astype(jnp.bfloat16).astype(jnp.float32)
    middle = (column - high).astype(jnp.bfloat16).astype(jnp.float32)
    return high, middle, column - high - middle


def pack(sums, squares):
    lane = lax.broadcasted_iota(jnp.int32, (sums.shape[0], LANES), 1)
    packed = jnp.zeros((sums.shape[0], LANES), jnp.float32)
    for at, piece in enumerate(pieces(sums) + pieces(squares)):
        packed = jnp.where(lane == at, piece, packed)
    return packed.astype(jnp.bfloat16)


def unpack(packed):
    packed = packed.astype(jnp.float32)
    column = [packed[:, at:at + 1] for at in range(6)]
    return column[0] + column[1] + column[2], column[3] + column[4] + column[5]


def pack_row(row_of, width, scratch, out_ref):
    count = width // LANES
    scratch[...] = jnp.zeros_like(scratch)
    for at in range(count):
        piece = row_of(at * LANES)
        high = piece.astype(jnp.bfloat16).astype(jnp.float32)
        for place, value in ((at, high), (count + at, piece - high)):
            group, line = divmod(place, scratch.shape[0])
            scratch[line:line + 1, group * LANES:(group + 1) * LANES] = value
    out_ref[...] = scratch[...].astype(jnp.bfloat16)


def unpack_row(packed, start, stop, width):
    count = width // LANES
    pieces = []
    for at in range(start // LANES, stop // LANES):
        piece = 0
        for place in (at, count + at):
            group, line = divmod(place, packed.shape[0])
            piece = piece + packed[line:line + 1, group * LANES:(group + 1) * LANES]
        pieces.append(piece)
    return jnp.concatenate(pieces, axis=1)


def load_kernel(start, weight_ref, out_ref, sem):
    copy = pltpu.make_async_copy(weight_ref.at[:, pl.ds(start, out_ref.shape[1])], out_ref, sem)
    copy.start()
    copy.wait()


def load_rest_kernel(gain_ref, first_ref, weight_ref, *refs):
    outs, (row_ref, packed_ref, scratch, sems) = refs[:-4], refs[-4:]
    width = first_ref.shape[1]
    tile = tile_of(width)
    tiles = range(0, width, tile)
    copies = {}
    for part, out_ref in enumerate(outs, 1):
        for at in tiles:
            copy = pltpu.make_async_copy(
                weight_ref.at[:, pl.ds(part * width + at, tile)],
                out_ref.at[:, pl.ds(at, tile)],
                sems.at[len(copies)],
            )
            copy.start()
            copies[part, at] = copy
    gain = gain_ref[...][None, :]
    high = gain.astype(jnp.bfloat16).astype(jnp.float32)
    row = lax.broadcasted_iota(jnp.int32, (16, gain.shape[1]), 0)
    rows = jnp.where(row == 0, high, jnp.where(row == 1, gain - high, 0.0)).astype(jnp.bfloat16)
    for part, loaded in enumerate((first_ref,) + outs):
        for at in tiles:
            if part:
                copies[part, at].wait()
            product = jnp.dot(rows, loaded[:, at:at + tile], preferred_element_type=jnp.float32)
            row_ref[:, part * width + at:part * width + at + tile] = product[0:1] + product[1:2]
    pack_row(lambda at: row_ref[:, at:at + LANES], row_ref.shape[1], scratch, packed_ref)


def up_kernel(near_ref, far_ref, gain_ref, packed_ref, weight_ref, rows_ref, own_ref, kept_ref, given_ref):
    half, block_width = near_ref.shape
    width = kept_ref.shape[1]
    first = is_first_core()
    near, far = near_ref[...].astype(jnp.float32), far_ref[...].astype(jnp.float32)
    for at, values in enumerate((jnp.where(first, near, far), jnp.where(first, far, near))):
        sums = jnp.sum(values, axis=1, keepdims=True)
        squares = jnp.sum(values * values, axis=1, keepdims=True)
        centred = (values - sums / block_width) * gain_ref[...][None, :]
        rows_ref[at * half:(at + 1) * half] = centred.astype(jnp.bfloat16)
        packed = pack(sums, squares)
        if at == 0:
            own_ref[...] = packed
        else:
            given_ref[:, width:width + LANES] = packed
    given_ref[:, width + LANES:] = packed_ref[...]
    up_products(rows_ref, weight_ref, kept_ref, given_ref)


def up_products(rows_ref, weight_ref, kept_ref, given_ref):
    half, width = kept_ref.shape
    tile = tile_of(width)
    for at in range(0, width, tile):
        product = jnp.dot(
            rows_ref[...], weight_ref[:, at:at + tile], preferred_element_type=jnp.float32
        )
        kept_ref[:, at:at + tile] = product[:half]
        given_ref[:, at:at + tile] = product[half:].astype(jnp.bfloat16)


def pair_kernel(start, full, block_width, kept_ref, own_ref, gain_ref, packed_ref, other_ref, sum_ref, sent_ref, scratch):
    width = kept_ref.shape[1]
    side = other_ref if start == 0 else packed_ref
    sums, squares = unpack(own_ref[...])
    other_sums, other_squares = unpack(side[:, width:width + LANES])
    shift = (sums - other_sums) / (2 * block_width)
    scratch[...] = side[:, width + LANES:].astype(jnp.float32)
    tile = tile_of(width)
    for at in range(0, width, tile):
        cut, there = slice(at, at + tile), slice(start + at, start + at + tile)
        gains = gain_ref[:, there] - unpack_row(scratch, there.start, there.stop, full)
        total = kept_ref[:, cut] + other_ref[:, cut].astype(jnp.float32) + shift * gains
        sum_ref[:, cut] = total
        sent_ref[:, cut] = total.astype(jnp.bfloat16)
    if start == 0:
        sent_ref[:, width:width + LANES] = pack(sums + other_sums, squares + other_squares)
        rows = [gain_ref[:, at:at + LANES] + unpack_row(scratch, at, at + LANES, full) for at in range(0, full, LANES)]
        pack_row(lambda at: rows[at // LANES], full, scratch, sent_ref.at[:, width + LANES:])


def gelu_kernel(start, full, block_width, full_width, peers, bias_ref, sum_ref, *refs):
    out_ref, scratch = refs[-2:]
    packed, others = refs[:peers + 1], refs[peers + 1:-2] or refs[1:peers + 1]
    width = sum_ref.shape[1]
    stats = [unpack(ref[:, width:width + LANES]) for ref in packed]
    row_mean = sum(s[0] for s in stats) / full_width
    spread = sum(s[1] for s in stats) / full_width - row_mean * row_mean
    scale = lax.rsqrt(spread + epsilon)
    shifts = [s[0] / (2 * block_width) - row_mean for s in stats]
    for at, ref in enumerate(packed):
        scratch[at] = ref[:, width + LANES:].astype(jnp.float32)
    tile = tile_of(width)
    for at in range(0, width, tile):
        cut, there = slice(at, at + tile), slice(start + at, start + at + tile)
        total = sum_ref[:, cut]
        for other in others:
            total = total + other[:, cut].astype(jnp.float32)
        for at, shift in enumerate(shifts):
            total = total + shift * unpack_row(scratch.at[at], there.start, there.stop, full)
        active = jax.nn.gelu(total * scale + bias_ref[:, there], approximate=True)
        out_ref[:, cut] = active.astype(jnp.bfloat16)


def down_kernel(start, last, kept_ref, given_ref, weight_ref, *refs):
    half, depth = kept_ref.shape
    rows_ref = refs[-1]
    rows_ref[:half] = kept_ref[...]
    rows_ref[half:] = given_ref[...]
    first = is_first_core()
    width = weight_ref.shape[1]
    tile = tile_of(width)
    for at in range(0, width, tile):
        cut = slice(at, at + tile)
        product = jnp.dot(
            rows_ref[...], weight_ref[start:start + depth, cut], preferred_element_type=jnp.float32
        )
        if start:
            product = product + refs[0][:, cut]
        if last:
            kept, given = product[:half], product[half:]
            refs[-3][:, cut] = jnp.where(first, kept, given)
            refs[-2][:, cut] = jnp.where(first, given, kept).astype(jnp.bfloat16)
        else:
            refs[-2][:, cut] = product


def per_device(
    patches, frame_counts, patch_mask, norm_gain, up_weight, up_bias, down_weight, down_bias
):
    tok_rows, block_width = patches.shape
    hidden_width = up_weight.shape[1]
    tok_size = lax.axis_size("tok")
    feat_size = lax.axis_size("feat")
    full_width = block_width * feat_size
    f32, bf16 = jnp.float32, jnp.bfloat16

    parts = PARTS if hidden_width % (PARTS * LANES) == 0 else 1
    width = hidden_width // parts
    starts = range(0, hidden_width, width)

    masks = range(2, tok_size, 2)
    peers = range(2, feat_size, 2)
    half = tok_rows * tok_size // 2
    side = LANES * -(-2 * hidden_width // (LANES * half))
    extra = [LANES + side if start == 0 else 0 for start in starts]
    copied = pltpu.SemaphoreType.DMA
    (loaded,) = call(
        functools.partial(load_kernel, 0),
        [((block_width, width), bf16)],
        [in_hbm],
        [copied],
        limit=46,
    )(up_weight)
    far_first = list(reversed(masks))
    order = [0] + far_first[1:2] + far_first[:1] + far_first[2:]
    near = jnp.concatenate([patches] + [swap(patches, "tok", mask) for mask in order[1:]])
    near, loaded, norm_gain = lax.optimization_barrier((near, loaded, norm_gain))
    far = swap(near, "tok", 1)
    *rest, gain_row, gain_packed = call(
        load_rest_kernel,
        [((block_width, width), bf16)] * (parts - 1)
        + [((1, hidden_width), f32), ((half, side), bf16)],
        [in_vmem] * 2 + [in_hbm],
        [
            pltpu.VMEM((half, side), f32),
            copied(((parts - 1) * (width // tile_of(width)) or 1,)),
        ],
        flops=32 * up_weight.size,
        limit=40,
    )(norm_gain, loaded, up_weight)
    loaded = [loaded, *rest]

    kepts, givens = [], []
    for start, more, weight in zip(starts, extra, loaded):
        outs = [((half, width), f32), ((half, width + more), bf16)]
        flops = 4 * half * block_width * width
        if start == 0:
            rows, own, kept, given = call(
                up_kernel,
                [((2 * half, block_width), bf16), ((half, LANES), bf16)] + outs,
                [in_vmem] * 5,
                flops=flops,
            )(near, far, norm_gain, gain_packed, weight)
        else:
            kept, given = call(
                up_products, outs, [in_vmem] * 2, flops=flops
            )(rows, weight)
        kepts.append(kept)
        givens.append(given)
    others = [swap(given, "feat", 1) for given in givens]
    sums, sents = [], []
    for start, more, kept, other in zip(starts, extra, kepts, others):
        pair_sum, sent = call(
            functools.partial(pair_kernel, start, hidden_width, block_width),
            [((half, width), f32), ((half, width + more), bf16)],
            [in_vmem] * 5,
            [pltpu.VMEM((half, side), f32)],
        )(kept, own, gain_row, others[0], other)
        sums.append(pair_sum)
        sents.append(sent)
    arrived = [[swap(sent, "feat", mask) for mask in peers] for sent in sents]
    total = ()
    for start, pair_sum, partners in zip(starts, sums, arrived):
        partners = partners if start else []
        (active,) = call(
            functools.partial(gelu_kernel, start, hidden_width, block_width, full_width, len(peers)),
            [((half, width), bf16)],
            [in_vmem] * (3 + len(peers) + len(partners)),
            [pltpu.VMEM((1 + len(peers), half, side), f32)],
        )(up_bias[None, :], pair_sum, sents[0], *arrived[0], *partners)
        last = start == starts[-1]
        total = call(
            functools.partial(down_kernel, start, last),
            [((half, block_width), f32), ((half, block_width), bf16)]
            if last
            else [((2 * half, block_width), f32)],
            [in_vmem] * (3 + len(total)),
            [pltpu.VMEM((2 * half, width), bf16)],
            flops=4 * half * width * block_width,
        )(active, swap(active, "feat", 1), down_weight, *total)
    near_sum, far_sum = total

    def rows_of(array, masks):
        at = [order.index(mask) * tok_rows for mask in masks]
        return jnp.concatenate([array[start:start + tok_rows] for start in at])

    first, second = far_first[:len(order) // 2], far_first[len(order) // 2:] + [0]
    summed = 0
    for group in (first, second):
        total = rows_of(near_sum, group) + swap(rows_of(far_sum, group), "tok", 1)
        for at, mask in enumerate(group):
            block = total[at * tok_rows:(at + 1) * tok_rows]
            summed = summed + (swap(block.astype(bf16), "tok", mask) if mask else block)

    positions = jnp.arange(tok_rows, dtype=jnp.int32)
    valid_rows = ((positions // FRAME_TOK < frame_counts) & (patch_mask == 1)).astype(f32)
    return (valid_rows[:, None] * (summed + down_bias[None, :])).astype(bf16)


def solution(mesh):
    in_specs = (
        P("tok", "feat"),
        P("tok"),
        P("tok"),
        P("feat"),
        P("feat", "tok"),
        P("tok"),
        P("tok", "feat"),
        P("feat"),
    )
    out_specs = P("tok", "feat")
    return jax.shard_map(
        per_device, mesh=mesh, in_specs=in_specs, out_specs=out_specs, check_vma=False
    )
```

```python
import functools

import jax
import jax.numpy as jnp
from jax import lax
from jax.experimental import pallas as pl
from jax.experimental.pallas import tpu as pltpu
from jax.sharding import PartitionSpec as P

FRAME_TOK = 4
LANES = 128
MIB = 2**20
PARTS = 3

epsilon = 1e-06

in_vmem = pl.BlockSpec(memory_space=pltpu.VMEM)
in_hbm = pl.BlockSpec(memory_space=pltpu.HBM)


def swap(block, axis, mask):
    size = lax.axis_size(axis)
    return lax.ppermute(block, axis, [(i, i ^ mask) for i in range(size)])


def is_first_core():
    return lax.rem(lax.axis_index("feat"), 2) == 0


def tile_of(width):
    return next((t for t in (512, 384, 256, 128) if width % t == 0), width)


def call(kernel, outs, in_specs, scratch=(), flops=0, limit=4):
    outs = [jax.ShapeDtypeStruct(shape, dtype) for shape, dtype in outs]
    return pl.pallas_call(
        kernel,
        out_shape=outs,
        in_specs=in_specs,
        out_specs=[in_vmem] * len(outs),
        scratch_shapes=list(scratch),
        compiler_params=pltpu.CompilerParams(vmem_limit_bytes=limit * MIB),
        cost_estimate=pl.CostEstimate(
            flops=8 * flops, bytes_accessed=0, transcendentals=0
        ),
    )


def pieces(column):
    high = column.astype(jnp.bfloat16).astype(jnp.float32)
    middle = (column - high).astype(jnp.bfloat16).astype(jnp.float32)
    return high, middle, column - high - middle


def pack(sums, squares):
    lane = lax.broadcasted_iota(jnp.int32, (sums.shape[0], LANES), 1)
    packed = jnp.zeros((sums.shape[0], LANES), jnp.float32)
    for at, piece in enumerate(pieces(sums) + pieces(squares)):
        packed = jnp.where(lane == at, piece, packed)
    return packed.astype(jnp.bfloat16)


def unpack(packed):
    packed = packed.astype(jnp.float32)
    column = [packed[:, at:at + 1] for at in range(6)]
    return column[0] + column[1] + column[2], column[3] + column[4] + column[5]


def pack_row(row_of, width, scratch, out_ref):
    count = width // LANES
    scratch[...] = jnp.zeros_like(scratch)
    for at in range(count):
        piece = row_of(at * LANES)
        high = piece.astype(jnp.bfloat16).astype(jnp.float32)
        for place, value in ((at, high), (count + at, piece - high)):
            group, line = divmod(place, scratch.shape[0])
            scratch[line:line + 1, group * LANES:(group + 1) * LANES] = value
    out_ref[...] = scratch[...].astype(jnp.bfloat16)


def unpack_row(packed, start, stop, width):
    count = width // LANES
    pieces = []
    for at in range(start // LANES, stop // LANES):
        piece = 0
        for place in (at, count + at):
            group, line = divmod(place, packed.shape[0])
            piece = piece + packed[line:line + 1, group * LANES:(group + 1) * LANES]
        pieces.append(piece)
    return jnp.concatenate(pieces, axis=1)


def load_kernel(start, weight_ref, out_ref, sem):
    copy = pltpu.make_async_copy(weight_ref.at[:, pl.ds(start, out_ref.shape[1])], out_ref, sem)
    copy.start()
    copy.wait()


def load_rest_kernel(gain_ref, first_ref, weight_ref, *refs):
    outs, (row_ref, packed_ref, scratch, sems) = refs[:-4], refs[-4:]
    width = first_ref.shape[1]
    tile = tile_of(width)
    tiles = range(0, width, tile)
    copies = {}
    for part, out_ref in enumerate(outs, 1):
        for at in tiles:
            copy = pltpu.make_async_copy(
                weight_ref.at[:, pl.ds(part * width + at, tile)],
                out_ref.at[:, pl.ds(at, tile)],
                sems.at[len(copies)],
            )
            copy.start()
            copies[part, at] = copy
    gain = gain_ref[...][None, :]
    high = gain.astype(jnp.bfloat16).astype(jnp.float32)
    row = lax.broadcasted_iota(jnp.int32, (16, gain.shape[1]), 0)
    rows = jnp.where(row == 0, high, jnp.where(row == 1, gain - high, 0.0)).astype(jnp.bfloat16)
    for part, loaded in enumerate((first_ref,) + outs):
        for at in tiles:
            if part:
                copies[part, at].wait()
            product = jnp.dot(rows, loaded[:, at:at + tile], preferred_element_type=jnp.float32)
            row_ref[:, part * width + at:part * width + at + tile] = product[0:1] + product[1:2]
    pack_row(lambda at: row_ref[:, at:at + LANES], row_ref.shape[1], scratch, packed_ref)


def up_kernel(near_ref, far_ref, gain_ref, packed_ref, weight_ref, rows_ref, own_ref, kept_ref, given_ref):
    half, block_width = near_ref.shape
    width = kept_ref.shape[1]
    first = is_first_core()
    near, far = near_ref[...].astype(jnp.float32), far_ref[...].astype(jnp.float32)
    for at, values in enumerate((jnp.where(first, near, far), jnp.where(first, far, near))):
        sums = jnp.sum(values, axis=1, keepdims=True)
        squares = jnp.sum(values * values, axis=1, keepdims=True)
        centred = (values - sums / block_width) * gain_ref[...][None, :]
        rows_ref[at * half:(at + 1) * half] = centred.astype(jnp.bfloat16)
        packed = pack(sums, squares)
        if at == 0:
            own_ref[...] = packed
        else:
            given_ref[:, width:width + LANES] = packed
    given_ref[:, width + LANES:] = packed_ref[...]
    up_products(rows_ref, weight_ref, kept_ref, given_ref)


def up_products(rows_ref, weight_ref, kept_ref, given_ref):
    half, width = kept_ref.shape
    tile = tile_of(width)
    for at in range(0, width, tile):
        product = jnp.dot(
            rows_ref[...], weight_ref[:, at:at + tile], preferred_element_type=jnp.float32
        )
        kept_ref[:, at:at + tile] = product[:half]
        given_ref[:, at:at + tile] = product[half:].astype(jnp.bfloat16)


def pair_kernel(start, full, block_width, kept_ref, own_ref, gain_ref, packed_ref, other_ref, sum_ref, sent_ref, scratch):
    width = kept_ref.shape[1]
    side = other_ref if start == 0 else packed_ref
    sums, squares = unpack(own_ref[...])
    other_sums, other_squares = unpack(side[:, width:width + LANES])
    shift = (sums - other_sums) / (2 * block_width)
    scratch[...] = side[:, width + LANES:].astype(jnp.float32)
    tile = tile_of(width)
    for at in range(0, width, tile):
        cut, there = slice(at, at + tile), slice(start + at, start + at + tile)
        gains = gain_ref[:, there] - unpack_row(scratch, there.start, there.stop, full)
        total = kept_ref[:, cut] + other_ref[:, cut].astype(jnp.float32) + shift * gains
        sum_ref[:, cut] = total
        sent_ref[:, cut] = total.astype(jnp.bfloat16)
    if start == 0:
        sent_ref[:, width:width + LANES] = pack(sums + other_sums, squares + other_squares)
        rows = [gain_ref[:, at:at + LANES] + unpack_row(scratch, at, at + LANES, full) for at in range(0, full, LANES)]
        pack_row(lambda at: rows[at // LANES], full, scratch, sent_ref.at[:, width + LANES:])


def gelu_kernel(start, full, block_width, full_width, peers, bias_ref, sum_ref, *refs):
    out_ref, scratch = refs[-2:]
    packed, others = refs[:peers + 1], refs[peers + 1:-2] or refs[1:peers + 1]
    width = sum_ref.shape[1]
    stats = [unpack(ref[:, width:width + LANES]) for ref in packed]
    row_mean = sum(s[0] for s in stats) / full_width
    spread = sum(s[1] for s in stats) / full_width - row_mean * row_mean
    scale = lax.rsqrt(spread + epsilon)
    shifts = [s[0] / (2 * block_width) - row_mean for s in stats]
    for at, ref in enumerate(packed):
        scratch[at] = ref[:, width + LANES:].astype(jnp.float32)
    tile = tile_of(width)
    for at in range(0, width, tile):
        cut, there = slice(at, at + tile), slice(start + at, start + at + tile)
        total = sum_ref[:, cut]
        for other in others:
            total = total + other[:, cut].astype(jnp.float32)
        for at, shift in enumerate(shifts):
            total = total + shift * unpack_row(scratch.at[at], there.start, there.stop, full)
        active = jax.nn.gelu(total * scale + bias_ref[:, there], approximate=True)
        out_ref[:, cut] = active.astype(jnp.bfloat16)


def down_kernel(start, count, last, *refs):
    actives, weight_ref, refs = refs[:2 * count], refs[2 * count], refs[2 * count + 1:]
    half, width = actives[0].shape
    rows_ref = refs[-1]
    for part in range(count):
        cut = slice(part * width, (part + 1) * width)
        rows_ref[:half, cut] = actives[2 * part][...]
        rows_ref[half:, cut] = actives[2 * part + 1][...]
    first = is_first_core()
    tile = tile_of(weight_ref.shape[1])
    for at in range(0, weight_ref.shape[1], tile):
        cut = slice(at, at + tile)
        product = jnp.dot(
            rows_ref[...], weight_ref[start:start + count * width, cut], preferred_element_type=jnp.float32
        )
        if start:
            product = product + refs[0][:, cut]
        if last:
            kept, given = product[:half], product[half:]
            refs[-3][:, cut] = jnp.where(first, kept, given)
            refs[-2][:, cut] = jnp.where(first, given, kept).astype(jnp.bfloat16)
        else:
            refs[-2][:, cut] = product


def per_device(
    patches, frame_counts, patch_mask, norm_gain, up_weight, up_bias, down_weight, down_bias
):
    tok_rows, block_width = patches.shape
    hidden_width = up_weight.shape[1]
    tok_size = lax.axis_size("tok")
    feat_size = lax.axis_size("feat")
    full_width = block_width * feat_size
    f32, bf16 = jnp.float32, jnp.bfloat16

    parts = PARTS if hidden_width % (PARTS * LANES) == 0 else 1
    width = hidden_width // parts
    starts = range(0, hidden_width, width)

    masks = range(2, tok_size, 2)
    peers = range(2, feat_size, 2)
    half = tok_rows * tok_size // 2
    side = LANES * -(-2 * hidden_width // (LANES * half))
    extra = [LANES + side if start == 0 else 0 for start in starts]
    copied = pltpu.SemaphoreType.DMA
    (loaded,) = call(
        functools.partial(load_kernel, 0),
        [((block_width, width), bf16)],
        [in_hbm],
        [copied],
        limit=46,
    )(up_weight)
    far_first = list(reversed(masks))
    order = [0] + far_first[1:2] + far_first[:1] + far_first[2:]
    near = jnp.concatenate([patches] + [swap(patches, "tok", mask) for mask in order[1:]])
    near, loaded, norm_gain = lax.optimization_barrier((near, loaded, norm_gain))
    far = swap(near, "tok", 1)
    *rest, gain_row, gain_packed = call(
        load_rest_kernel,
        [((block_width, width), bf16)] * (parts - 1)
        + [((1, hidden_width), f32), ((half, side), bf16)],
        [in_vmem] * 2 + [in_hbm],
        [
            pltpu.VMEM((half, side), f32),
            copied(((parts - 1) * (width // tile_of(width)) or 1,)),
        ],
        flops=32 * up_weight.size,
        limit=40,
    )(norm_gain, loaded, up_weight)
    loaded = [loaded, *rest]

    kepts, givens = [], []
    for start, more, weight in zip(starts, extra, loaded):
        outs = [((half, width), f32), ((half, width + more), bf16)]
        flops = 4 * half * block_width * width
        if start == 0:
            rows, own, kept, given = call(
                up_kernel,
                [((2 * half, block_width), bf16), ((half, LANES), bf16)] + outs,
                [in_vmem] * 5,
                flops=flops,
            )(near, far, norm_gain, gain_packed, weight)
        else:
            kept, given = call(
                up_products, outs, [in_vmem] * 2, flops=flops
            )(rows, weight)
        kepts.append(kept)
        givens.append(given)
    others = [swap(given, "feat", 1) for given in givens]
    sums, sents = [], []
    for start, more, kept, other in zip(starts, extra, kepts, others):
        pair_sum, sent = call(
            functools.partial(pair_kernel, start, hidden_width, block_width),
            [((half, width), f32), ((half, width + more), bf16)],
            [in_vmem] * 5,
            [pltpu.VMEM((half, side), f32)],
        )(kept, own, gain_row, others[0], other)
        sums.append(pair_sum)
        sents.append(sent)
    arrived = [[swap(sent, "feat", mask) for mask in peers] for sent in sents]
    total, actives = (), {}
    for start, pair_sum, partners in zip(starts, sums, arrived):
        partners = partners if start else []
        (active,) = call(
            functools.partial(gelu_kernel, start, hidden_width, block_width, full_width, len(peers)),
            [((half, width), bf16)],
            [in_vmem] * (3 + len(peers) + len(partners)),
            [pltpu.VMEM((1 + len(peers), half, side), f32)],
        )(up_bias[None, :], pair_sum, sents[0], *arrived[0], *partners)
        actives[start] = (active, swap(active, "feat", 1))
    for group in (starts[:-1], starts[-1:]):
        last = starts[-1] in group
        if len(group) > 0:
            total = call(
                functools.partial(down_kernel, group[0], len(group), last),
                [((half, block_width), f32), ((half, block_width), bf16)]
                if last
                else [((2 * half, block_width), f32)],
                [in_vmem] * (2 * len(group) + 1 + len(total)),
                [pltpu.VMEM((2 * half, len(group) * width), bf16)],
                flops=4 * half * len(group) * width * block_width,
            )(*[block for start in group for block in actives[start]], down_weight, *total)
    near_sum, far_sum = total

    def rows_of(array, masks):
        at = [order.index(mask) * tok_rows for mask in masks]
        return jnp.concatenate([array[start:start + tok_rows] for start in at])

    first, second = far_first[:len(order) // 2], far_first[len(order) // 2:] + [0]
    summed = 0
    for group in (first, second):
        total = rows_of(near_sum, group) + swap(rows_of(far_sum, group), "tok", 1)
        for at, mask in enumerate(group):
            block = total[at * tok_rows:(at + 1) * tok_rows]
            summed = summed + (swap(block.astype(bf16), "tok", mask) if mask else block)

    positions = jnp.arange(tok_rows, dtype=jnp.int32)
    valid_rows = ((positions // FRAME_TOK < frame_counts) & (patch_mask == 1)).astype(f32)
    return (valid_rows[:, None] * (summed + down_bias[None, :])).astype(bf16)


def solution(mesh):
    in_specs = (
        P("tok", "feat"),
        P("tok"),
        P("tok"),
        P("feat"),
        P("feat", "tok"),
        P("tok"),
        P("tok", "feat"),
        P("feat"),
    )
    out_specs = P("tok", "feat")
    return jax.shard_map(
        per_device, mesh=mesh, in_specs=in_specs, out_specs=out_specs, check_vma=False
    )
```
